256 devices in a mesh: req: 64 (over y_lo, x, z), tp: 4 (over y_hi, core).
Axes of the slice: x: 4, y: 4 (y_hi: 2, y_lo: 2; y = y_hi * 2 + y_lo), z: 8, core: 2. Of those that a mesh axis runs over, the one named last changes fastest.
Arguments:
- queries: bfloat16 [4096, 4, 4096], P('req', None, 'tp'), may hold values from -64 to 64
- prefix_keys: bfloat16 [4096, 512], P('req', 'tp'), may hold values from -6 to 6
- prefix_values: bfloat16 [4096, 512], P('req', 'tp'), may hold values from -6 to 6
- suffix_keys: bfloat16 [4096, 64, 512], P('req', None, 'tp'), may hold values from -9 to 9
- suffix_values: bfloat16 [4096, 64, 512], P('req', None, 'tp'), may hold values from -6 to 6
- new_keys: bfloat16 [4096, 4, 512], P('req', None, 'tp'), may hold values from -15 to 15
- new_values: bfloat16 [4096, 4, 512], P('req', None, 'tp'), may hold values from -6 to 6
- suffix_lengths: int32 [4096], P('req'), may hold values from 1 to 64, as said below
- out_weight: bfloat16 [4096, 4096], P('tp'), may hold values from -0.09375 to 0.09375
Outputs:
- attended: bfloat16 [4096, 4, 4096], P('req')
The draws below stay inside these ranges and needn't reach their ends.
Inputs may be any that keep to these rules, and one draw needn't show every extreme that they name: `suffix_lengths`: some request has all 64 slots live.
All inputs are finite; a program needn't handle non-finite values.
Results may differ from the reference program's by a relative error of at most 0.015.
Values may be sent and summed in bfloat16 or wider, within the bound.
No kernel may reach another device: no remote copies, remote signals or barrier semaphores. Data moves between devices by JAX's collectives and lax.ppermute only.
A program may use at most 128 MiB of HBM per device.

```python
import math
import jax
import jax.numpy as jnp
from jax import lax

D = 4096
NH = 32
KVH = 4
HD = 128
STEPS = 4
REQ_DEV = 64
SUFFIX = 64
REQUESTS = 4096
PREFIX = 4096


def draw_queries(key, part):
    key = jax.random.fold_in(key, 1)
    key_noise = jax.random.fold_in(key, 0)
    noise = jnp.clip(jax.random.normal(key_noise, (REQUESTS, STEPS, NH * HD), jnp.float32), -6.0, 6.0)
    values = 2.0 * noise
    return values.astype(jnp.bfloat16)


def draw_prefix_keys(key, part):
    key = jax.random.fold_in(key, 2)
    values = jnp.clip(jax.random.normal(key, (PREFIX, KVH, HD), jnp.float32), -6.0, 6.0)
    return values.reshape(PREFIX, KVH * HD).astype(jnp.bfloat16)


def draw_suffix_lengths(key, part):
    key = jax.random.fold_in(key, 3)
    key_lengths, key_index = jax.random.split(key, 2)
    lengths = jax.random.randint(key_lengths, (REQUESTS,), 1, SUFFIX + 1)
    index = jax.random.randint(key_index, (), 0, REQUESTS)
    return lengths.at[index].set(SUFFIX).astype(jnp.int32)


def steps_of(rng, shape, pieces, smallest, high):
    loudness, own = 1.0, jax.random.fold_in(rng, 6)
    for position, blocks in pieces:
        steps = jnp.exp(jax.random.uniform(jax.random.fold_in(own, position), (blocks,), jnp.float32, smallest / len(pieces), high / len(pieces)))
        loudness = loudness * jnp.repeat(steps, shape[position] // blocks).reshape([-1 if axis == position else 1 for axis in range(len(shape))])
    return loudness


def normal_values(key, extent, width, most, cuts=(), kind=jnp.bfloat16):
    array = jax.random.normal(key, extent, jnp.float32) * width
    if len(cuts) > 0:
        array = steps_of(key, extent, cuts, -0.22, 0.18) * array
    return jnp.clip(array, min=-most, max=most).astype(kind)


def setup_inputs(seed: int = 0) -> dict:
    key_list = jax.random.split(jax.random.key(seed), 10)
    queries = draw_queries(jax.random.fold_in(key_list[9], 71), 0)
    prefix_keys = draw_prefix_keys(jax.random.fold_in(key_list[9], 71), 0)
    prefix_values = normal_values(key_list[2], (PREFIX, KVH * HD), 1.0, 6.0, ((0, 64), (1, 4)))
    suffix_keys = normal_values(key_list[3], (REQUESTS, SUFFIX, KVH * HD), 1.5, 9.0, ((0, 64), (2, 4)))
    suffix_values = normal_values(key_list[4], (REQUESTS, SUFFIX, KVH * HD), 1.0, 6.0, ((0, 64), (2, 4)))
    new_keys = normal_values(key_list[5], (REQUESTS, STEPS, KVH * HD), 2.5, 15.0, ((0, 64), (2, 4)))
    new_values = normal_values(key_list[6], (REQUESTS, STEPS, KVH * HD), 1.0, 6.0, ((0, 64), (2, 4)))
    suffix_lengths = draw_suffix_lengths(jax.random.fold_in(key_list[9], 71), 0)
    out_weight = normal_values(key_list[8], (NH * HD, D), (NH * HD) ** -0.5, 0.09375, ((0, 4),))
    return {"queries": queries, "prefix_keys": prefix_keys, "prefix_values": prefix_values, "suffix_keys": suffix_keys, "suffix_values": suffix_values, "new_keys": new_keys, "new_values": new_values, "suffix_lengths": suffix_lengths, "out_weight": out_weight}


def reference(queries, prefix_keys, prefix_values, suffix_keys, suffix_values, new_keys, new_values, suffix_lengths, out_weight):
    group = NH // KVH
    scale = 1.0 / math.sqrt(HD)
    block = REQ_DEV
    count = REQUESTS // block
    high = lax.Precision.HIGHEST
    pre_keys = prefix_keys.astype(jnp.float32).reshape(PREFIX, KVH, HD)
    pre_vals = prefix_values.astype(jnp.float32).reshape(PREFIX, KVH, HD)

    def one_block(items):
        qry, s_keys, s_vals, n_keys, n_vals, lengths = items
        qry = qry.astype(jnp.float32).reshape(block, STEPS, KVH, group, HD)
        s_keys = s_keys.astype(jnp.float32).reshape(block, SUFFIX, KVH, HD)
        s_vals = s_vals.astype(jnp.float32).reshape(block, SUFFIX, KVH, HD)
        n_keys = n_keys.astype(jnp.float32).reshape(block, STEPS, KVH, HD)
        n_vals = n_vals.astype(jnp.float32).reshape(block, STEPS, KVH, HD)
        s_pre = jnp.einsum('btkgd,pkd->btkgp', qry, pre_keys, precision=high) * scale
        s_suf = jnp.einsum('btkgd,bskd->btkgs', qry, s_keys, precision=high) * scale
        live = jnp.arange(SUFFIX)[None, :] < lengths[:, None]
        s_suf = jnp.where(live[:, None, None, None, :], s_suf, -jnp.inf)
        s_new = jnp.einsum('btkgd,bukd->btkgu', qry, n_keys, precision=high) * scale
        causal = jnp.arange(STEPS)[None, :] <= jnp.arange(STEPS)[:, None]
        s_new = jnp.where(causal[None, :, None, None, :], s_new, -jnp.inf)
        scores = jnp.concatenate([s_pre, s_suf, s_new], axis=-1)
        maxima = lax.optimization_barrier(jnp.max(scores, axis=-1, keepdims=True))
        exps = jnp.exp(scores - maxima)
        totals = lax.optimization_barrier(jnp.sum(exps, axis=-1))
        rounded = lax.optimization_barrier(exps.astype(jnp.bfloat16)).astype(jnp.float32)
        out = jnp.einsum('btkgp,pkd->btkgd', rounded[..., :PREFIX], pre_vals, precision=high)
        out = out + jnp.einsum('btkgs,bskd->btkgd', rounded[..., PREFIX:PREFIX + SUFFIX], s_vals, precision=high)
        out = out + jnp.einsum('btkgu,bukd->btkgd', rounded[..., PREFIX + SUFFIX:], n_vals, precision=high)
        out = out / totals[..., None]
        heads_out = out.reshape(block * STEPS, NH * HD).astype(jnp.bfloat16)
        result = jnp.dot(heads_out, out_weight, preferred_element_type=jnp.float32)
        return result.astype(jnp.bfloat16).reshape(block, STEPS, D)
    items = (queries.reshape(count, block, STEPS, NH * HD), suffix_keys.reshape(count, block, SUFFIX, KVH * HD), suffix_values.reshape(count, block, SUFFIX, KVH * HD), new_keys.reshape(count, block, STEPS, KVH * HD), new_values.reshape(count, block, STEPS, KVH * HD), suffix_lengths.reshape(count, block))
    return lax.map(one_block, items).reshape(REQUESTS, STEPS, D)
```

```python
import math

import jax
import jax.numpy as jnp
from jax import lax
from jax.experimental import pallas as pl
from jax.experimental.pallas import tpu as pltpu
from jax.sharding import Mesh, PartitionSpec as P

HD = 128
GROUP = 8
STEPS = 4
SLOTS = 64
TOK = 16
PACK = TOK * GROUP
SCALE = math.log2(math.e) / math.sqrt(HD)
LOW = -1e30

E_PAIRS = [(i, i ^ 1) for i in range(8)]
O_PAIRS = [(i, (i + 1) % 8 if i % 2 else (i - 1) % 8) for i in range(8)]


def dot_t(a, b):
    return lax.dot_general(a, b, (((1,), (1,)), ((), ())), preferred_element_type=jnp.float32)


def dot(a, b):
    return jnp.dot(a, b, preferred_element_type=jnp.float32)


def with_ones(v):
    return jnp.concatenate([v, jnp.ones_like(v)], axis=1)


def row_max(s):
    return jnp.max(s, axis=1, keepdims=True)


def suffix_body(q_ref, sk_ref, sv_ref, nk_ref, nv_ref, bias_ref, qp_ref, m_ref, acc_ref):
    packs = q_ref.shape[0] // TOK
    keys = TOK // STEPS * SLOTS
    row = lax.broadcasted_iota(jnp.int32, (PACK, keys), 0)
    col = lax.broadcasted_iota(jnp.int32, (PACK, keys), 1)
    same = ((row >> 2) & 3) == (col >> 6)
    row_n = lax.broadcasted_iota(jnp.int32, (PACK, TOK), 0)
    col_n = lax.broadcasted_iota(jnp.int32, (PACK, TOK), 1)
    same_n = (((row_n >> 2) & 3) == (col_n >> 2)) & ((col_n & 3) <= (row_n & 3))
    for g in range(packs):
        block = q_ref[g * TOK : (g + 1) * TOK, :]
        q = jnp.concatenate([block[:, h * HD : (h + 1) * HD] for h in range(GROUP)], axis=0)
        rows = pl.ds(g * PACK, PACK)
        qp_ref[rows, :] = q
        k = sk_ref[g * keys : (g + 1) * keys, :]
        v = sv_ref[g * keys : (g + 1) * keys, :]
        s = dot_t(q, k) * SCALE + bias_ref[g]
        s = jnp.where(same, s, LOW)
        s_n = dot_t(q, nk_ref[g * TOK : (g + 1) * TOK, :]) * SCALE
        s_n = jnp.where(same_n, s_n, LOW)
        m = jnp.maximum(row_max(s), row_max(s_n))
        p = jnp.exp2(s - m).astype(jnp.bfloat16)
        p_n = jnp.exp2(s_n - m).astype(jnp.bfloat16)
        acc = dot(p, with_ones(v)) + dot(p_n, with_ones(nv_ref[g * TOK : (g + 1) * TOK, :]))
        m_ref[rows, :] = jnp.broadcast_to(m, (PACK, HD))
        acc_ref[rows, :] = acc


def suffix(q, sk, sv, nk, nv, bias):
    rows = q.shape[0] * GROUP
    grid = 4
    part = lambda a: pl.BlockSpec((a.shape[0] // grid,) + a.shape[1:], lambda i: (i,) + (0,) * (a.ndim - 1))
    outs = [
        jax.ShapeDtypeStruct((rows, HD), jnp.bfloat16),
        jax.ShapeDtypeStruct((rows, HD), jnp.float32),
        jax.ShapeDtypeStruct((rows, 2 * HD), jnp.float32),
    ]
    return pl.pallas_call(
        suffix_body,
        grid=(grid,),
        in_specs=[part(a) for a in (q, sk, sv, nk, nv, bias)],
        out_specs=[part(o) for o in outs],
        out_shape=outs,
        cost_estimate=pl.CostEstimate(flops=300_000_000, bytes_accessed=6_000_000, transcendentals=600_000),
        compiler_params=pltpu.CompilerParams(vmem_limit_bytes=24 * 1024 * 1024),
        name="suffix",
    )(q, sk, sv, nk, nv, bias)


def step(q, m, acc, kvs):
    parts = [dot_t(q, kv[:, :HD]) for kv in kvs]
    top = row_max(parts[0])
    for s in parts[1:]:
        top = jnp.maximum(top, row_max(s))
    new = jnp.maximum(m, top * SCALE)
    acc = acc * jnp.exp2(m - new)[:, :1]
    for s, kv in zip(parts, kvs):
        p = jnp.exp2(s * SCALE - new[:, :1]).astype(jnp.bfloat16)
        acc = acc + dot(p, with_ones(kv[:, HD:]))
    return new, acc


def prefix_body(n, *refs):
    q_ref, m_ref, acc_ref = refs[:3]
    m_out, acc_out = refs[3 + n :]
    new, acc = step(q_ref[...], m_ref[...], acc_ref[...], [r[...] for r in refs[3 : 3 + n]])
    m_out[...] = new
    acc_out[...] = acc


def final_body(n, *refs):
    q_ref, m_ref, acc_ref = refs[:3]
    out_ref = refs[3 + n]
    _, acc = step(q_ref[...], m_ref[...], acc_ref[...], [r[...] for r in refs[3 : 3 + n]])
    heads = (acc[:, :HD] / acc[:, HD:]).astype(jnp.bfloat16)
    for g in range(heads.shape[0] // PACK):
        for h in range(GROUP):
            first = g * PACK + h * TOK
            out_ref[g * TOK : (g + 1) * TOK, h * HD : (h + 1) * HD] = heads[first : first + TOK, :]


def prefix(q, m, acc, kvs, tile=256):
    rows = q.shape[0]
    part = lambda a: pl.BlockSpec((tile, a.shape[1]), lambda i: (i, 0))
    whole = lambda a: pl.BlockSpec(a.shape, lambda i: (0, 0))
    keys = sum(kv.shape[0] for kv in kvs)
    return pl.pallas_call(
        lambda *refs: prefix_body(len(kvs), *refs),
        grid=(rows // tile,),
        in_specs=[part(q), part(m), part(acc)] + [whole(kv) for kv in kvs],
        out_specs=[part(m), part(acc)],
        out_shape=[jax.ShapeDtypeStruct(m.shape, m.dtype), jax.ShapeDtypeStruct(acc.shape, acc.dtype)],
        cost_estimate=pl.CostEstimate(flops=rows * keys * HD * 8, bytes_accessed=7_000_000, transcendentals=rows * keys),
        compiler_params=pltpu.CompilerParams(vmem_limit_bytes=24 * 1024 * 1024),
        name="prefix",
    )(q, m, acc, *kvs)


def final(q, m, acc, kvs, chunk, chunks, tile=256):
    rows = q.shape[0] // chunks
    steps = rows // tile
    part = lambda a: pl.BlockSpec((tile, a.shape[1]), lambda i: (i + chunk * steps, 0))
    whole = lambda a: pl.BlockSpec(a.shape, lambda i: (0, 0))
    keys = sum(kv.shape[0] for kv in kvs)
    return pl.pallas_call(
        lambda *refs: final_body(len(kvs), *refs),
        grid=(steps,),
        in_specs=[part(q), part(m), part(acc)] + [whole(kv) for kv in kvs],
        out_specs=pl.BlockSpec((tile // GROUP, GROUP * HD), lambda i: (i, 0)),
        out_shape=jax.ShapeDtypeStruct((rows // GROUP, GROUP * HD), jnp.bfloat16),
        cost_estimate=pl.CostEstimate(flops=rows * keys * HD * 8, bytes_accessed=2_000_000, transcendentals=rows * keys),
        compiler_params=pltpu.CompilerParams(vmem_limit_bytes=24 * 1024 * 1024),
        name="final",
    )(q, m, acc, *kvs)


def local(queries, prefix_keys, prefix_values, suffix_keys, suffix_values, new_keys, new_values, suffix_lengths, out_weight):
    requests = queries.shape[0]
    tokens = requests * STEPS
    half = out_weight.shape[1] // 2
    core = lax.axis_index("core")
    even = lambda a: lax.ppermute(a, "z", E_PAIRS)
    odd = lambda a: lax.ppermute(a, "z", O_PAIRS)
    x1 = lambda a: lax.ppermute(a, "x", [(i, i ^ 1) for i in range(4)])
    x3 = lambda a: lax.ppermute(a, "x", [(i, i ^ 3) for i in range(4)])
    y = lambda a: lax.ppermute(a, "ylo", [(0, 1), (1, 0)])
    swap_core = lambda a: lax.ppermute(a, "core", [(0, 1), (1, 0)])
    swap_y = lambda a: lax.ppermute(a, "yhi", [(0, 1), (1, 0)])

    kv = jnp.concatenate([prefix_keys, prefix_values], axis=1)
    pair = jnp.concatenate([kv, even(kv)], axis=0)
    r2 = odd(pair)
    r3 = even(r2)
    r4 = odd(r3)
    line = jnp.concatenate([pair, r2, r3, r4], axis=0)
    b_x1, b_x3, b_y = x1(line), x3(line), y(line)
    b_yx1, b_yx3 = x1(b_y), x3(b_y)
    b_far = x1(b_x3)
    b_yfar = x3(b_yx1)

    weight_mine = lax.dynamic_slice(out_weight, (0, core * half), (out_weight.shape[0], half))
    weight_other = swap_core(lax.dynamic_slice(out_weight, (0, (1 - core) * half), (out_weight.shape[0], half)))

    flat = lambda a: a.reshape(-1, a.shape[-1])
    live = jnp.arange(SLOTS)[None, :] < suffix_lengths[:, None]
    bias = jnp.where(live, 0.0, LOW).astype(jnp.float32).reshape(tokens // TOK, 1, TOK // STEPS * SLOTS)
    q, m, acc = suffix(flat(queries), flat(suffix_keys), flat(suffix_values), flat(new_keys), flat(new_values), bias)
    m, acc = prefix(q, m, acc, [line])
    m, acc = prefix(q, m, acc, [b_x1, b_x3, b_y])
    m, acc = prefix(q, m, acc, [b_yx1, b_yx3])
    chunks = 4
    results = []
    for chunk in range(chunks):
        mine = final(q, m, acc, [b_far, b_yfar], chunk, chunks)
        other = swap_core(mine)
        terms = dot(mine, weight_mine) + dot(other, weight_other)
        total = (terms + swap_y(terms.astype(jnp.bfloat16)).astype(jnp.float32)).astype(jnp.bfloat16)
        rest = swap_core(total)
        left = jnp.where(core == 0, total, rest)
        right = jnp.where(core == 0, rest, total)
        results.append(jnp.concatenate([left, right], axis=1).reshape(requests // chunks, STEPS, 2 * half))
    return jnp.concatenate(results, axis=0)


def solution(mesh):
    fine = Mesh(mesh.devices.reshape(2, 4, 8, 2, 2), ("ylo", "x", "z", "yhi", "core"))
    req, tp = ("ylo", "x", "z"), ("yhi", "core")
    in_specs = (
        P(req, None, tp),
        P(req, tp),
        P(req, tp),
        P(req, None, tp),
        P(req, None, tp),
        P(req, None, tp),
        P(req, None, tp),
        P(req),
        P(tp, None),
    )
    return jax.shard_map(local, mesh=fine, in_specs=in_specs, out_specs=P(req, None, None), check_vma=False)
```

```python
import math

import jax
import jax.numpy as jnp
from jax import lax
from jax.experimental import pallas as pl
from jax.experimental.pallas import tpu as pltpu
from jax.sharding import Mesh, PartitionSpec as P

HD = 128
GROUP = 8
STEPS = 4
SLOTS = 64
TOK = 16
PACK = TOK * GROUP
SCALE = math.log2(math.e) / math.sqrt(HD)
LOW = -1e30
MIB = 1024 * 1024

E_PAIRS = [(i, i ^ 1) for i in range(8)]
O_PAIRS = [(i, (i + 1) % 8 if i % 2 else (i - 1) % 8) for i in range(8)]


def dot_t(a, b):
    return lax.dot_general(a, b, (((1,), (1,)), ((), ())), preferred_element_type=jnp.float32)


def dot(a, b):
    return jnp.dot(a, b, preferred_element_type=jnp.float32)


def with_ones(v):
    return jnp.concatenate([v, jnp.ones_like(v)], axis=1)


def wide(a, count):
    return jnp.concatenate([a] * count, axis=1) if count > 1 else a


def row_max(s):
    top = s[:, :HD]
    for j in range(HD, s.shape[1], HD):
        top = jnp.maximum(top, s[:, j : j + HD])
    return jnp.max(top, axis=1, keepdims=True)


def join_body(k_ref, v_ref, out_ref, sem):
    copies = [
        pltpu.make_async_copy(k_ref, out_ref.at[:, :HD], sem.at[0]),
        pltpu.make_async_copy(v_ref, out_ref.at[:, HD:], sem.at[1]),
    ]
    for copy in copies:
        copy.start()
    for copy in copies:
        copy.wait()


def join(k, v):
    return pl.pallas_call(
        join_body,
        in_specs=[pl.BlockSpec(memory_space=pltpu.HBM)] * 2,
        out_specs=pl.BlockSpec(memory_space=pltpu.VMEM),
        out_shape=jax.ShapeDtypeStruct((k.shape[0], 2 * HD), k.dtype),
        scratch_shapes=[pltpu.SemaphoreType.DMA((2,))],
        compiler_params=pltpu.CompilerParams(vmem_limit_bytes=60 * MIB),
        name="join",
    )(k, v)


def suffix_body(q_ref, nk_ref, nv_ref, sk_all, sv_all, len_ref, qp_ref, m_ref, acc_ref, sk_held, sv_held, sem):
    packs = q_ref.shape[0] // TOK
    base = pl.program_id(0) * packs
    per = TOK // STEPS
    keys = per * SLOTS
    now = pl.program_id(0)
    block = packs * keys

    def fetch(i):
        rows = pl.ds(pl.multiple_of(i * block, block), block)
        return [
            pltpu.make_async_copy(sk_all.at[rows, :], sk_held.at[i], sem.at[0, i]),
            pltpu.make_async_copy(sv_all.at[rows, :], sv_held.at[i], sem.at[1, i]),
        ]

    @pl.when(now == 0)
    def _():
        for i in range(sk_held.shape[0]):
            for copy in fetch(i):
                copy.start()

    for copy in fetch(now):
        copy.wait()
    sk_ref, sv_ref = sk_held.at[now], sv_held.at[now]
    row = lax.broadcasted_iota(jnp.int32, (PACK, keys), 0)
    col = lax.broadcasted_iota(jnp.int32, (PACK, keys), 1)
    owner = (row >> 2) & 3
    same = owner == (col >> 6)
    slot = col & (SLOTS - 1)
    row_n = lax.broadcasted_iota(jnp.int32, (PACK, TOK), 0)
    col_n = lax.broadcasted_iota(jnp.int32, (PACK, TOK), 1)
    same_n = (((row_n >> 2) & 3) == (col_n >> 2)) & ((col_n & 3) <= (row_n & 3))

    def scores(g):
        block = q_ref[g * TOK : (g + 1) * TOK, :]
        q = jnp.concatenate([block[:, h * HD : (h + 1) * HD] for h in range(GROUP)], axis=0)
        qp_ref[g * PACK : (g + 1) * PACK, :] = q
        return dot_t(q, sk_ref[g * keys : (g + 1) * keys, :]), dot_t(q, nk_ref[g * TOK : (g + 1) * TOK, :])

    ahead = scores(0)
    for g in range(packs):
        s, s_n = ahead
        if g + 1 < packs:
            ahead = scores(g + 1)
        rows = pl.ds(g * PACK, PACK)
        length = jnp.full((PACK, keys), len_ref[(base + g) * per], jnp.int32)
        for j in range(1, per):
            length = jnp.where(owner == j, len_ref[(base + g) * per + j], length)
        s = jnp.where(same & (slot < length), s * SCALE, LOW)
        s_n = jnp.where(same_n, s_n * SCALE, LOW)
        m = jnp.maximum(row_max(s), jnp.max(s_n, axis=1, keepdims=True))
        p = jnp.exp2(s - m).astype(jnp.bfloat16)
        p_n = jnp.exp2(s_n - m).astype(jnp.bfloat16)
        new_v = nv_ref[g * TOK : (g + 1) * TOK, :]
        m_ref[rows, :] = jnp.broadcast_to(m, (PACK, HD))
        acc_ref[rows, :] = dot(p, with_ones(sv_ref[g * keys : (g + 1) * keys, :])) + dot(p_n, with_ones(new_v))


def suffix(q, sk, sv, nk, nv, lengths):
    rows = q.shape[0] * GROUP
    grid = 4
    part = lambda a: pl.BlockSpec((a.shape[0] // grid, a.shape[1]), lambda i: (i, 0))
    outs = [
        jax.ShapeDtypeStruct((rows, HD), jnp.bfloat16),
        jax.ShapeDtypeStruct((rows, HD), jnp.float32),
        jax.ShapeDtypeStruct((rows, 2 * HD), jnp.float32),
    ]
    return pl.pallas_call(
        suffix_body,
        grid=(grid,),
        in_specs=[part(a) for a in (q, nk, nv)]
        + [pl.BlockSpec(memory_space=pltpu.HBM)] * 2
        + [pl.BlockSpec(memory_space=pltpu.SMEM)],
        out_specs=[part(o) for o in outs],
        out_shape=outs,
        scratch_shapes=[pltpu.VMEM((grid, sk.shape[0] // grid, HD), jnp.bfloat16)] * 2 + [pltpu.SemaphoreType.DMA((2, grid))],
        cost_estimate=pl.CostEstimate(flops=300_000_000, bytes_accessed=6_000_000, transcendentals=600_000),
        compiler_params=pltpu.CompilerParams(vmem_limit_bytes=12 * MIB),
        name="suffix",
    )(q, nk, nv, sk, sv, lengths)


def attend(q, m, acc, kvs, emit, tile=256):
    tiles = q.shape[0] // tile
    scores = lambda i: [dot_t(q[i * tile : (i + 1) * tile, :], kv[:, :HD]) for kv in kvs]
    ahead = scores(0)
    for i in range(tiles):
        parts = ahead
        if i + 1 < tiles:
            ahead = scores(i + 1)
        rows = slice(i * tile, (i + 1) * tile)
        top = row_max(parts[0])
        for s in parts[1:]:
            top = jnp.maximum(top, row_max(s))
        old = m[rows, :]
        new = jnp.maximum(old, top * SCALE)
        out = acc[rows, :] * wide(jnp.exp2(old - new), 2)
        for s, kv in zip(parts, kvs):
            p = jnp.exp2(s * SCALE - wide(new, s.shape[1] // HD)).astype(jnp.bfloat16)
            out = out + dot(p, with_ones(kv[:, HD:]))
        emit(i, rows, new, out)


def prefix_body(n, *refs):
    m_out, acc_out = refs[3 + n :]

    def emit(_, rows, new, out):
        m_out[rows, :] = new
        acc_out[rows, :] = out

    attend(refs[0], refs[1], refs[2], refs[3 : 3 + n], emit)


def prefix(q, m, acc, kvs, tile=1024):
    rows = q.shape[0]
    part = lambda a: pl.BlockSpec((tile, a.shape[1]), lambda i: (i, 0))
    whole = lambda a: pl.BlockSpec(a.shape, lambda i: (0, 0))
    keys = sum(kv.shape[0] for kv in kvs)
    return pl.pallas_call(
        lambda *refs: prefix_body(len(kvs), *refs),
        grid=(rows // tile,),
        in_specs=[part(q), part(m), part(acc)] + [whole(kv) for kv in kvs],
        out_specs=[part(m), part(acc)],
        out_shape=[jax.ShapeDtypeStruct(m.shape, m.dtype), jax.ShapeDtypeStruct(acc.shape, acc.dtype)],
        cost_estimate=pl.CostEstimate(flops=rows * keys * HD * 8, bytes_accessed=7_000_000, transcendentals=rows * keys),
        compiler_params=pltpu.CompilerParams(vmem_limit_bytes=16 * MIB),
        name="prefix",
    )(q, m, acc, *kvs)


def final_body(n, *refs):
    weight_ref = refs[3 + n]
    mine_ref, other_ref, heads_ref = refs[4 + n :]

    def emit(i, rows, _, out):
        heads = (out[:, :HD] / out[:, HD:]).astype(jnp.bfloat16)
        packs = heads.shape[0] // PACK
        for g in range(packs):
            for h in range(GROUP):
                first = g * PACK + h * TOK
                to = (i * packs + g) * TOK
                heads_ref[to : to + TOK, h * HD : (h + 1) * HD] = heads[first : first + TOK, :]

    attend(refs[0], refs[1], refs[2], refs[3 : 3 + n], emit)
    heads = heads_ref[...]
    requests, steps, half = mine_ref.shape
    core = lax.axis_index("core")
    width = 512
    for ref, side in ((other_ref, 1 - core), (mine_ref, core)):
        for j in range(0, half, width):
            columns = pl.ds(pl.multiple_of(side * half + j, width), width)
            terms = dot(heads, weight_ref[:, columns])
            ref[:, :, j : j + width] = terms.reshape(requests, steps, width).astype(ref.dtype)


def final(q, m, acc, kvs, weight):
    rows = q.shape[0]
    tokens, half = rows // GROUP, weight.shape[1] // 2
    keys = sum(kv.shape[0] for kv in kvs)
    whole = lambda a: pl.BlockSpec(a.shape, lambda i: (0,) * len(a.shape))
    shape = (tokens // STEPS, STEPS, half)
    outs = [jax.ShapeDtypeStruct(shape, jnp.float32), jax.ShapeDtypeStruct(shape, jnp.bfloat16)]
    return pl.pallas_call(
        lambda *refs: final_body(len(kvs), *refs),
        grid=(1,),
        in_specs=[whole(a) for a in (q, m, acc, *kvs)] + [pl.BlockSpec(memory_space=pltpu.VMEM)],
        out_specs=[whole(o) for o in outs],
        out_shape=outs,
        scratch_shapes=[pltpu.VMEM((tokens, GROUP * HD), jnp.bfloat16)],
        cost_estimate=pl.CostEstimate(
            flops=rows * keys * HD * 8 + 8 * tokens * weight.size, bytes_accessed=12_000_000, transcendentals=rows * keys
        ),
        compiler_params=pltpu.CompilerParams(vmem_limit_bytes=24 * MIB),
        name="final",
    )(q, m, acc, *kvs, weight)


def place_body(n, lows, *refs):
    out_ref, sem = refs[-2:]
    half = refs[0].shape[2]
    core = lax.axis_index("core")
    copies = []
    for i in range(n):
        side = core if i % 2 == 0 else 1 - core
        rows = pl.ds(lows[i // 2], refs[i].shape[0])
        columns = pl.ds(pl.multiple_of(side * half, half), half)
        copies.append(pltpu.make_async_copy(refs[i], out_ref.at[rows, :, columns], sem.at[i]))
    for copy in copies:
        copy.start()
    for copy in copies:
        copy.wait()


def place(pieces, lows, shape, out=None):
    n = len(pieces)
    return pl.pallas_call(
        lambda *refs: place_body(n, lows, *refs),
        in_specs=[pl.BlockSpec(memory_space=pltpu.VMEM)] * n + ([] if out is None else [pl.BlockSpec(memory_space=pl.ANY)]),
        out_specs=pl.BlockSpec(memory_space=pl.ANY),
        out_shape=jax.ShapeDtypeStruct(shape, pieces[0].dtype),
        scratch_shapes=[pltpu.SemaphoreType.DMA((n,))],
        input_output_aliases={} if out is None else {n: 0},
        compiler_params=pltpu.CompilerParams(vmem_limit_bytes=2 * MIB),
        name="place",
    )(*pieces, *([] if out is None else [out]))


def local(queries, prefix_keys, prefix_values, suffix_keys, suffix_values, new_keys, new_values, suffix_lengths, out_weight):
    requests = queries.shape[0]
    even = lambda a: lax.ppermute(a, "z", E_PAIRS)
    odd = lambda a: lax.ppermute(a, "z", O_PAIRS)
    x1 = lambda a: lax.ppermute(a, "x", [(i, i ^ 1) for i in range(4)])
    x3 = lambda a: lax.ppermute(a, "x", [(i, i ^ 3) for i in range(4)])
    y = lambda a: lax.ppermute(a, "ylo", [(0, 1), (1, 0)])
    swap_core = lambda a: lax.ppermute(a, "core", [(0, 1), (1, 0)])
    swap_y = lambda a: lax.ppermute(a, "yhi", [(0, 1), (1, 0)])

    flat = lambda a: a.reshape(-1, a.shape[-1])
    args = [flat(a) for a in (queries, suffix_keys, suffix_values, new_keys, new_values)]

    kv = join(prefix_keys, prefix_values)
    pair = jnp.concatenate([kv, even(kv)], axis=0)
    r2 = odd(pair)
    r3 = even(r2)
    r4 = odd(r3)
    line = jnp.concatenate([pair, r2, r3, r4], axis=0)
    b_x1, b_x3, b_y = x1(line), x3(line), y(line)
    b_yx1, b_yx3 = x1(b_y), x3(b_y)
    b_far = x1(b_x3)
    b_yfar = x3(b_yx1)

    q, m, acc = suffix(*args, suffix_lengths)
    m, acc = prefix(q, m, acc, [line])
    m, acc = prefix(q, m, acc, [b_x1, b_x3, b_y])
    m, acc = prefix(q, m, acc, [b_yx1, b_yx3])
    mine, other = final(q, m, acc, [b_far, b_yfar], out_weight)
    terms = (mine + swap_core(other).astype(jnp.float32)).astype(jnp.bfloat16)
    sizes = (16, 16, 16, 8, 8)
    lows = [sum(sizes[:i]) for i in range(len(sizes))]
    pieces = [terms[low : low + size] for low, size in zip(lows, sizes)]
    moved = [swap_y(piece) for piece in pieces]
    halves = []
    for piece, got in zip(pieces, moved):
        total = piece + got
        halves += [total, swap_core(total)]
    shape = (requests, STEPS, out_weight.shape[1])
    early = 2 * (len(sizes) - 1)
    out = place(halves[:early], lows[:-1], shape)
    return place(halves[early:], lows[-1:], shape, out)


def solution(mesh):
    fine = Mesh(mesh.devices.reshape(2, 4, 8, 2, 2), ("ylo", "x", "z", "yhi", "core"))
    req, tp = ("ylo", "x", "z"), ("yhi", "core")
    in_specs = (
        P(req, None, tp),
        P(req, tp),
        P(req, tp),
        P(req, None, tp),
        P(req, None, tp),
        P(req, None, tp),
        P(req, None, tp),
        P(req),
        P(tp, None),
    )
    return jax.shard_map(local, mesh=fine, in_specs=in_specs, out_specs=P(req, None, None), check_vma=False)
```

```python
import math

import jax
import jax.numpy as jnp
from jax import lax
from jax.experimental import pallas as pl
from jax.experimental.pallas import tpu as pltpu
from jax.sharding import Mesh, PartitionSpec as P

HD = 128
GROUP = 8
STEPS = 4
SLOTS = 64
TOK = 16
PACK = TOK * GROUP
SCALE = math.log2(math.e) / math.sqrt(HD)
LOW = -1e30
MIB = 1024 * 1024

E_PAIRS = [(i, i ^ 1) for i in range(8)]
O_PAIRS = [(i, (i + 1) % 8 if i % 2 else (i - 1) % 8) for i in range(8)]


def dot_t(a, b):
    return lax.dot_general(a, b, (((1,), (1,)), ((), ())), preferred_element_type=jnp.float32)


def dot(a, b):
    return jnp.dot(a, b, preferred_element_type=jnp.float32)


def with_ones(v):
    return jnp.concatenate([v, jnp.ones_like(v)], axis=1)


def wide(a, count):
    return jnp.concatenate([a] * count, axis=1) if count > 1 else a


def row_max(s):
    top = s[:, :HD]
    for j in range(HD, s.shape[1], HD):
        top = jnp.maximum(top, s[:, j : j + HD])
    return jnp.max(top, axis=1, keepdims=True)


def join_body(k_ref, v_ref, got_k_ref, got_v_ref, out_ref):
    rows = k_ref.shape[0]
    out_ref[:rows, :HD] = k_ref[...]
    out_ref[:rows, HD:] = v_ref[...]
    out_ref[rows:, :HD] = got_k_ref[...]
    out_ref[rows:, HD:] = got_v_ref[...]


def join(k, v, got_k, got_v):
    return pl.pallas_call(
        join_body,
        out_shape=jax.ShapeDtypeStruct((2 * k.shape[0], 2 * HD), k.dtype),
        cost_estimate=pl.CostEstimate(flops=10_000_000_000, bytes_accessed=200_000, transcendentals=0),
        compiler_params=pltpu.CompilerParams(vmem_limit_bytes=MIB),
        name="join",
    )(k, v, got_k, got_v)


def suffix_body(q_ref, nk_ref, nv_ref, sk_all, sv_all, len_ref, _, qp_ref, m_ref, acc_ref, sk_held, sv_held, sem):
    packs = q_ref.shape[0] * STEPS // TOK
    base = pl.program_id(0) * packs
    per = TOK // STEPS
    keys = per * SLOTS
    now = pl.program_id(0)
    block = packs * keys

    def fetch(i):
        rows = pl.ds(pl.multiple_of(i * block, block), block)
        return [
            pltpu.make_async_copy(sk_all.at[rows, :], sk_held.at[i], sem.at[0, i]),
            pltpu.make_async_copy(sv_all.at[rows, :], sv_held.at[i], sem.at[1, i]),
        ]

    @pl.when(now == 0)
    def _():
        for i in range(sk_held.shape[0]):
            for copy in fetch(i):
                copy.start()

    for copy in fetch(now):
        copy.wait()
    sk_ref, sv_ref = sk_held.at[now], sv_held.at[now]
    row = lax.broadcasted_iota(jnp.int32, (PACK, keys), 0)
    col = lax.broadcasted_iota(jnp.int32, (PACK, keys), 1)
    owner = (row >> 2) & 3
    same = owner == (col >> 6)
    slot = col & (SLOTS - 1)
    row_n = lax.broadcasted_iota(jnp.int32, (PACK, TOK), 0)
    col_n = lax.broadcasted_iota(jnp.int32, (PACK, TOK), 1)
    same_n = (((row_n >> 2) & 3) == (col_n >> 2)) & ((col_n & 3) <= (row_n & 3))

    def scores(g):
        block = q_ref[g * per : (g + 1) * per, :, :].astype(jnp.float32)
        block = block.reshape(TOK, GROUP * HD).astype(jnp.bfloat16)
        q = jnp.concatenate([block[:, h * HD : (h + 1) * HD] for h in range(GROUP)], axis=0)
        qp_ref[g * PACK : (g + 1) * PACK, :] = q
        return dot_t(q, sk_ref[g * keys : (g + 1) * keys, :]), dot_t(q, nk_ref[g * TOK : (g + 1) * TOK, :])

    ahead = scores(0)
    for g in range(packs):
        s, s_n = ahead
        if g + 1 < packs:
            ahead = scores(g + 1)
        rows = pl.ds(g * PACK, PACK)
        length = jnp.full((PACK, keys), len_ref[(base + g) * per], jnp.int32)
        for j in range(1, per):
            length = jnp.where(owner == j, len_ref[(base + g) * per + j], length)
        s = jnp.where(same & (slot < length), s * SCALE, LOW)
        s_n = jnp.where(same_n, s_n * SCALE, LOW)
        m = jnp.maximum(row_max(s), jnp.max(s_n, axis=1, keepdims=True))
        p = jnp.exp2(s - m).astype(jnp.bfloat16)
        p_n = jnp.exp2(s_n - m).astype(jnp.bfloat16)
        new_v = nv_ref[g * TOK : (g + 1) * TOK, :]
        m_ref[rows, :] = jnp.broadcast_to(m, (PACK, HD))
        acc_ref[rows, :] = dot(p, with_ones(sv_ref[g * keys : (g + 1) * keys, :])) + dot(p_n, with_ones(new_v))


def suffix(q, sk, sv, nk, nv, lengths, after):
    rows = q.shape[0] * STEPS * GROUP
    grid = 4
    part = lambda a: pl.BlockSpec((a.shape[0] // grid,) + a.shape[1:], lambda i: (i,) + (0,) * (len(a.shape) - 1))
    outs = [
        jax.ShapeDtypeStruct((rows, HD), jnp.bfloat16),
        jax.ShapeDtypeStruct((rows, HD), jnp.float32),
        jax.ShapeDtypeStruct((rows, 2 * HD), jnp.float32),
    ]
    return pl.pallas_call(
        suffix_body,
        grid=(grid,),
        in_specs=[part(a) for a in (q, nk, nv)]
        + [pl.BlockSpec(memory_space=pltpu.HBM)] * 2
        + [pl.BlockSpec(memory_space=pltpu.SMEM), pl.BlockSpec(memory_space=pl.ANY)],
        out_specs=[part(o) for o in outs],
        out_shape=outs,
        scratch_shapes=[pltpu.VMEM((grid, sk.shape[0] // grid, HD), jnp.bfloat16)] * 2 + [pltpu.SemaphoreType.DMA((2, grid))],
        cost_estimate=pl.CostEstimate(flops=4_000_000_000, bytes_accessed=6_000_000, transcendentals=600_000),
        compiler_params=pltpu.CompilerParams(vmem_limit_bytes=12 * MIB),
        name="suffix",
    )(q, nk, nv, sk, sv, lengths, after)


def attend(q, m, acc, kvs, emit, tile=256):
    tiles = q.shape[0] // tile
    scores = lambda i: [dot_t(q[i * tile : (i + 1) * tile, :], kv[:, :HD]) for kv in kvs]
    ahead = scores(0)
    for i in range(tiles):
        parts = ahead
        if i + 1 < tiles:
            ahead = scores(i + 1)
        rows = slice(i * tile, (i + 1) * tile)
        top = row_max(parts[0])
        for s in parts[1:]:
            top = jnp.maximum(top, row_max(s))
        old = m[rows, :]
        new = jnp.maximum(old, top * SCALE)
        out = acc[rows, :] * wide(jnp.exp2(old - new), 2)
        for s, kv in zip(parts, kvs):
            p = jnp.exp2(s * SCALE - wide(new, s.shape[1] // HD)).astype(jnp.bfloat16)
            out = out + dot(p, with_ones(kv[:, HD:]))
        emit(i, rows, new, out)


def prefix_body(n, *refs):
    m_out, acc_out = refs[3 + n :]

    def emit(_, rows, new, out):
        m_out[rows, :] = new
        acc_out[rows, :] = out

    attend(refs[0], refs[1], refs[2], refs[3 : 3 + n], emit)


def prefix(q, m, acc, kvs, tile=1024):
    rows = q.shape[0]
    part = lambda a: pl.BlockSpec((tile, a.shape[1]), lambda i: (i, 0))
    whole = lambda a: pl.BlockSpec(a.shape, lambda i: (0, 0))
    keys = sum(kv.shape[0] for kv in kvs)
    return pl.pallas_call(
        lambda *refs: prefix_body(len(kvs), *refs),
        grid=(rows // tile,),
        in_specs=[part(q), part(m), part(acc)] + [whole(kv) for kv in kvs],
        out_specs=[part(m), part(acc)],
        out_shape=[jax.ShapeDtypeStruct(m.shape, m.dtype), jax.ShapeDtypeStruct(acc.shape, acc.dtype)],
        cost_estimate=pl.CostEstimate(flops=rows * keys * HD * 8, bytes_accessed=7_000_000, transcendentals=rows * keys),
        compiler_params=pltpu.CompilerParams(vmem_limit_bytes=16 * MIB),
        name="prefix",
    )(q, m, acc, *kvs)


def final_body(n, *refs):
    weight_ref, mine_ref, other_ref, heads_ref = refs[3 + n :]

    def emit(i, rows, _, out):
        heads = (out[:, :HD] / out[:, HD:]).astype(jnp.bfloat16)
        packs = heads.shape[0] // PACK
        for g in range(packs):
            for h in range(GROUP):
                first = g * PACK + h * TOK
                to = (i * packs + g) * TOK
                heads_ref[to : to + TOK, h * HD : (h + 1) * HD] = heads[first : first + TOK, :]

    attend(refs[0], refs[1], refs[2], refs[3 : 3 + n], emit)
    heads = heads_ref[...]
    requests, steps, half = mine_ref.shape
    core = lax.axis_index("core")
    width = 512
    for ref, side in ((other_ref, 1 - core), (mine_ref, core)):
        for j in range(0, half, width):
            columns = pl.ds(pl.multiple_of(side * half + j, width), width)
            terms = dot(heads, weight_ref[:, columns])
            ref[:, :, j : j + width] = terms.reshape(requests, steps, width).astype(ref.dtype)


def final(q, m, acc, kvs, weight):
    rows = q.shape[0]
    tokens, half = rows // GROUP, weight.shape[1] // 2
    keys = sum(kv.shape[0] for kv in kvs)
    whole = lambda a: pl.BlockSpec(a.shape, lambda i: (0,) * len(a.shape))
    shape = (tokens // STEPS, STEPS, half)
    outs = [jax.ShapeDtypeStruct(shape, jnp.float32), jax.ShapeDtypeStruct(shape, jnp.bfloat16)]
    return pl.pallas_call(
        lambda *refs: final_body(len(kvs), *refs),
        grid=(1,),
        in_specs=[whole(a) for a in (q, m, acc, *kvs)] + [pl.BlockSpec(memory_space=pltpu.VMEM)],
        out_specs=[whole(o) for o in outs],
        out_shape=outs,
        scratch_shapes=[pltpu.VMEM((tokens, GROUP * HD), jnp.bfloat16)],
        cost_estimate=pl.CostEstimate(
            flops=rows * keys * HD * 8 + 8 * tokens * weight.size, bytes_accessed=12_000_000, transcendentals=rows * keys
        ),
        compiler_params=pltpu.CompilerParams(vmem_limit_bytes=24 * MIB),
        name="final",
    )(q, m, acc, *kvs, weight)


def place_body(n, lows, *refs):
    out_ref, sem = refs[-2:]
    half = refs[0].shape[2]
    core = lax.axis_index("core")
    copies = []
    for i in range(n):
        side = core if i % 2 == 0 else 1 - core
        rows = pl.ds(lows[i // 2], refs[i].shape[0])
        columns = pl.ds(pl.multiple_of(side * half, half), half)
        copies.append(pltpu.make_async_copy(refs[i], out_ref.at[rows, :, columns], sem.at[i]))
    for copy in copies:
        copy.start()
    for copy in copies:
        copy.wait()


def place(pieces, lows, shape):
    n = len(pieces)
    return pl.pallas_call(
        lambda *refs: place_body(n, lows, *refs),
        in_specs=[pl.BlockSpec(memory_space=pltpu.VMEM)] * n,
        out_specs=pl.BlockSpec(memory_space=pl.ANY),
        out_shape=jax.ShapeDtypeStruct(shape, pieces[0].dtype),
        scratch_shapes=[pltpu.SemaphoreType.DMA((n,))],
        compiler_params=pltpu.CompilerParams(vmem_limit_bytes=2 * MIB),
        name="place",
    )(*pieces)


def local(queries, prefix_keys, prefix_values, suffix_keys, suffix_values, new_keys, new_values, suffix_lengths, out_weight):
    requests = queries.shape[0]
    even = lambda a: lax.ppermute(a, "z", E_PAIRS)
    odd = lambda a: lax.ppermute(a, "z", O_PAIRS)
    x1 = lambda a: lax.ppermute(a, "x", [(i, i ^ 1) for i in range(4)])
    x3 = lambda a: lax.ppermute(a, "x", [(i, i ^ 3) for i in range(4)])
    y = lambda a: lax.ppermute(a, "ylo", [(0, 1), (1, 0)])
    swap_core = lambda a: lax.ppermute(a, "core", [(0, 1), (1, 0)])
    swap_y = lambda a: lax.ppermute(a, "yhi", [(0, 1), (1, 0)])

    flat = lambda a: a.reshape(-1, a.shape[-1])
    args = [queries] + [flat(a) for a in (suffix_keys, suffix_values, new_keys, new_values)]
    after = lambda a, b: lax.optimization_barrier((a, b))[0]

    pair = join(prefix_keys, prefix_values, even(prefix_keys), even(prefix_values))
    r2 = odd(pair)
    q, m, acc = suffix(*args, suffix_lengths, r2)
    r3 = after(even(r2), m)
    r4 = odd(r3)
    line = jnp.concatenate([pair, r2, r3, r4], axis=0)
    b_x1, b_x3, b_y = x1(line), x3(line), y(line)
    b_yx1, b_yx3 = x1(b_y), x3(b_y)
    b_far = x1(b_x3)
    b_yfar = x3(b_yx1)

    m, acc = prefix(q, m, acc, [line])
    m, acc = prefix(q, m, acc, [b_x1, b_x3, b_y])
    m, acc = prefix(q, m, acc, [b_yx1, b_yx3, b_far])

    mine, other = final(q, m, acc, [b_yfar], out_weight)
    terms = (mine + swap_core(other).astype(jnp.float32)).astype(jnp.bfloat16)
    shape = (requests, STEPS, out_weight.shape[1])
    cuts = (0, 16, 32, 48, 56, requests)
    pieces = [terms[low:high] for low, high in zip(cuts, cuts[1:])]
    halves = []
    for piece in pieces:
        total = piece + swap_y(piece)
        halves += [total, swap_core(total)]
    return place(halves, cuts[:-1], shape)


def solution(mesh):
    fine = Mesh(mesh.devices.reshape(2, 4, 8, 2, 2), ("ylo", "x", "z", "yhi", "core"))
    req, tp = ("ylo", "x", "z"), ("yhi", "core")
    in_specs = (
        P(req, None, tp),
        P(req, tp),
        P(req, tp),
        P(req, None, tp),
        P(req, None, tp),
        P(req, None, tp),
        P(req, None, tp),
        P(req),
        P(tp, None),
    )
    return jax.shard_map(local, mesh=fine, in_specs=in_specs, out_specs=P(req, None, None), check_vma=False)
```

```python
import math

import jax
import jax.numpy as jnp
from jax import lax
from jax.experimental import pallas as pl
from jax.experimental.pallas import tpu as pltpu
from jax.sharding import Mesh, PartitionSpec as P

HD = 128
GROUP = 8
STEPS = 4
SLOTS = 64
TOK = 16
PACK = TOK * GROUP
SCALE = math.log2(math.e) / math.sqrt(HD)
LOW = -1e30
MIB = 1024 * 1024

E_PAIRS = [(i, i ^ 1) for i in range(8)]
O_PAIRS = [(i, (i + 1) % 8 if i % 2 else (i - 1) % 8) for i in range(8)]


def dot_t(a, b):
    return lax.dot_general(a, b, (((1,), (1,)), ((), ())), preferred_element_type=jnp.float32)


def dot(a, b):
    return jnp.dot(a, b, preferred_element_type=jnp.float32)


def with_ones(v):
    return jnp.concatenate([v, jnp.ones_like(v)], axis=1)


def wide(a, count):
    return jnp.concatenate([a] * count, axis=1) if count > 1 else a


def row_max(s):
    top = s[:, :HD]
    for j in range(HD, s.shape[1], HD):
        top = jnp.maximum(top, s[:, j : j + HD])
    return jnp.max(top, axis=1, keepdims=True)


def pack_body(k_ref, v_ref, out_ref):
    out_ref[:, :HD] = k_ref[...]
    out_ref[:, HD:] = v_ref[...]


def join_body(own_ref, k_ref, v_ref, out_ref):
    rows = k_ref.shape[0]
    out_ref[:rows, :] = own_ref[...]
    out_ref[rows:, :HD] = k_ref[...]
    out_ref[rows:, HD:] = v_ref[...]


def glue(body, rows, flops, *arrays):
    return pl.pallas_call(
        body,
        out_shape=jax.ShapeDtypeStruct((rows, 2 * HD), arrays[0].dtype),
        cost_estimate=pl.CostEstimate(flops=flops, bytes_accessed=200_000, transcendentals=0),
        compiler_params=pltpu.CompilerParams(vmem_limit_bytes=MIB),
        name="glue",
    )(*arrays)


def suffix_body(q_ref, nk_ref, nv_ref, sk_all, sv_all, len_ref, _, qp_ref, m_ref, acc_ref, sk_held, sv_held, sem):
    packs = q_ref.shape[0] * STEPS // TOK
    base = pl.program_id(0) * packs
    per = TOK // STEPS
    keys = per * SLOTS
    now = pl.program_id(0)
    block = packs * keys

    def fetch(i):
        rows = pl.ds(pl.multiple_of(i * block, block), block)
        return [
            pltpu.make_async_copy(sk_all.at[rows, :], sk_held.at[i], sem.at[0, i]),
            pltpu.make_async_copy(sv_all.at[rows, :], sv_held.at[i], sem.at[1, i]),
        ]

    @pl.when(now == 0)
    def _():
        for i in range(sk_held.shape[0]):
            for copy in fetch(i):
                copy.start()

    for copy in fetch(now):
        copy.wait()
    sk_ref, sv_ref = sk_held.at[now], sv_held.at[now]
    row = lax.broadcasted_iota(jnp.int32, (PACK, keys), 0)
    col = lax.broadcasted_iota(jnp.int32, (PACK, keys), 1)
    owner = (row >> 2) & 3
    same = owner == (col >> 6)
    slot = col & (SLOTS - 1)
    row_n = lax.broadcasted_iota(jnp.int32, (PACK, TOK), 0)
    col_n = lax.broadcasted_iota(jnp.int32, (PACK, TOK), 1)
    same_n = (((row_n >> 2) & 3) == (col_n >> 2)) & ((col_n & 3) <= (row_n & 3))

    def scores(g):
        block = q_ref[g * per : (g + 1) * per, :, :].astype(jnp.float32)
        block = block.reshape(TOK, GROUP * HD).astype(jnp.bfloat16)
        q = jnp.concatenate([block[:, h * HD : (h + 1) * HD] for h in range(GROUP)], axis=0)
        qp_ref[g * PACK : (g + 1) * PACK, :] = q
        return dot_t(q, sk_ref[g * keys : (g + 1) * keys, :]), dot_t(q, nk_ref[g * TOK : (g + 1) * TOK, :])

    ahead = scores(0)
    for g in range(packs):
        s, s_n = ahead
        if g + 1 < packs:
            ahead = scores(g + 1)
        rows = pl.ds(g * PACK, PACK)
        length = jnp.full((PACK, keys), len_ref[(base + g) * per], jnp.int32)
        for j in range(1, per):
            length = jnp.where(owner == j, len_ref[(base + g) * per + j], length)
        s = jnp.where(same & (slot < length), s * SCALE, LOW)
        s_n = jnp.where(same_n, s_n * SCALE, LOW)
        m = jnp.maximum(row_max(s), jnp.max(s_n, axis=1, keepdims=True))
        p = jnp.exp2(s - m).astype(jnp.bfloat16)
        p_n = jnp.exp2(s_n - m).astype(jnp.bfloat16)
        new_v = nv_ref[g * TOK : (g + 1) * TOK, :]
        m_ref[rows, :] = jnp.broadcast_to(m, (PACK, HD))
        acc_ref[rows, :] = dot(p, with_ones(sv_ref[g * keys : (g + 1) * keys, :])) + dot(p_n, with_ones(new_v))


def suffix(q, sk, sv, nk, nv, lengths, after):
    rows = q.shape[0] * STEPS * GROUP
    grid = 4
    part = lambda a: pl.BlockSpec((a.shape[0] // grid,) + a.shape[1:], lambda i: (i,) + (0,) * (len(a.shape) - 1))
    outs = [
        jax.ShapeDtypeStruct((rows, HD), jnp.bfloat16),
        jax.ShapeDtypeStruct((rows, HD), jnp.float32),
        jax.ShapeDtypeStruct((rows, 2 * HD), jnp.float32),
    ]
    return pl.pallas_call(
        suffix_body,
        grid=(grid,),
        in_specs=[part(a) for a in (q, nk, nv)]
        + [pl.BlockSpec(memory_space=pltpu.HBM)] * 2
        + [pl.BlockSpec(memory_space=pltpu.SMEM), pl.BlockSpec(memory_space=pl.ANY)],
        out_specs=[part(o) for o in outs],
        out_shape=outs,
        scratch_shapes=[pltpu.VMEM((grid, sk.shape[0] // grid, HD), jnp.bfloat16)] * 2 + [pltpu.SemaphoreType.DMA((2, grid))],
        cost_estimate=pl.CostEstimate(flops=4_000_000_000, bytes_accessed=6_000_000, transcendentals=600_000),
        compiler_params=pltpu.CompilerParams(vmem_limit_bytes=12 * MIB),
        name="suffix",
    )(q, nk, nv, sk, sv, lengths, after)


def attend(q, m, acc, kvs, emit, tile=256):
    tiles = q.shape[0] // tile
    scores = lambda i: [dot_t(q[i * tile : (i + 1) * tile, :], kv[:, :HD]) for kv in kvs]
    ahead = scores(0)
    for i in range(tiles):
        parts = ahead
        if i + 1 < tiles:
            ahead = scores(i + 1)
        rows = slice(i * tile, (i + 1) * tile)
        top = row_max(parts[0])
        for s in parts[1:]:
            top = jnp.maximum(top, row_max(s))
        old = m[rows, :]
        new = jnp.maximum(old, top * SCALE)
        out = acc[rows, :] * wide(jnp.exp2(old - new), 2)
        for s, kv in zip(parts, kvs):
            p = jnp.exp2(s * SCALE - wide(new, s.shape[1] // HD)).astype(jnp.bfloat16)
            out = out + dot(p, with_ones(kv[:, HD:]))
        emit(i, rows, new, out)


def prefix_body(n, *refs):
    m_out, acc_out = refs[3 + n :]

    def emit(_, rows, new, out):
        m_out[rows, :] = new
        acc_out[rows, :] = out

    attend(refs[0], refs[1], refs[2], refs[3 : 3 + n], emit)


def prefix(q, m, acc, kvs, tile=1024):
    rows = q.shape[0]
    part = lambda a: pl.BlockSpec((tile, a.shape[1]), lambda i: (i, 0))
    whole = lambda a: pl.BlockSpec(a.shape, lambda i: (0, 0))
    keys = sum(kv.shape[0] for kv in kvs)
    return pl.pallas_call(
        lambda *refs: prefix_body(len(kvs), *refs),
        grid=(rows // tile,),
        in_specs=[part(q), part(m), part(acc)] + [whole(kv) for kv in kvs],
        out_specs=[part(m), part(acc)],
        out_shape=[jax.ShapeDtypeStruct(m.shape, m.dtype), jax.ShapeDtypeStruct(acc.shape, acc.dtype)],
        cost_estimate=pl.CostEstimate(flops=rows * keys * HD * 8, bytes_accessed=7_000_000, transcendentals=rows * keys),
        compiler_params=pltpu.CompilerParams(vmem_limit_bytes=16 * MIB),
        name="prefix",
    )(q, m, acc, *kvs)


def final_body(n, *refs):
    weight_ref, mine_ref, head_ref, tail_ref, heads_ref = refs[3 + n :]
    low = head_ref.shape[0]

    def emit(i, rows, _, out):
        heads = (out[:, :HD] / out[:, HD:]).astype(jnp.bfloat16)
        packs = heads.shape[0] // PACK
        for g in range(packs):
            for h in range(GROUP):
                first = g * PACK + h * TOK
                to = (i * packs + g) * TOK
                heads_ref[to : to + TOK, h * HD : (h + 1) * HD] = heads[first : first + TOK, :]

    attend(refs[0], refs[1], refs[2], refs[3 : 3 + n], emit)
    heads = heads_ref[...]
    requests, steps, half = mine_ref.shape
    core = lax.axis_index("core")
    width = 512
    for side in (1 - core, core):
        for j in range(0, half, width):
            columns = pl.ds(pl.multiple_of(side * half + j, width), width)
            terms = dot(heads, weight_ref[:, columns]).reshape(requests, steps, width)
            if side is core:
                mine_ref[:, :, j : j + width] = terms
            else:
                terms = terms.astype(head_ref.dtype)
                head_ref[:, :, j : j + width] = terms[:low]
                tail_ref[:, :, j : j + width] = terms[low:]


def final(q, m, acc, kvs, weight, low):
    rows = q.shape[0]
    tokens, half = rows // GROUP, weight.shape[1] // 2
    keys = sum(kv.shape[0] for kv in kvs)
    whole = lambda a: pl.BlockSpec(a.shape, lambda i: (0,) * len(a.shape))
    requests = tokens // STEPS
    outs = [jax.ShapeDtypeStruct((requests, STEPS, half), jnp.float32)]
    outs += [jax.ShapeDtypeStruct((n, STEPS, half), jnp.bfloat16) for n in (low, requests - low)]
    return pl.pallas_call(
        lambda *refs: final_body(len(kvs), *refs),
        grid=(1,),
        in_specs=[whole(a) for a in (q, m, acc, *kvs)] + [pl.BlockSpec(memory_space=pltpu.VMEM)],
        out_specs=[whole(o) for o in outs],
        out_shape=outs,
        scratch_shapes=[pltpu.VMEM((tokens, GROUP * HD), jnp.bfloat16)],
        cost_estimate=pl.CostEstimate(
            flops=rows * keys * HD * 8 + 8 * tokens * weight.size, bytes_accessed=12_000_000, transcendentals=rows * keys
        ),
        compiler_params=pltpu.CompilerParams(vmem_limit_bytes=24 * MIB),
        name="final",
    )(q, m, acc, *kvs, weight)


def place_body(n, lows, *refs):
    out_ref, sem = refs[-2:]
    half = refs[0].shape[2]
    core = lax.axis_index("core")
    copies = []
    for i in range(n):
        side = core if i % 2 == 0 else 1 - core
        rows = pl.ds(lows[i // 2], refs[i].shape[0])
        columns = pl.ds(pl.multiple_of(side * half, half), half)
        copies.append(pltpu.make_async_copy(refs[i], out_ref.at[rows, :, columns], sem.at[i]))
    for copy in copies:
        copy.start()
    for copy in copies:
        copy.wait()


def place(pieces, lows, shape):
    n = len(pieces)
    return pl.pallas_call(
        lambda *refs: place_body(n, lows, *refs),
        in_specs=[pl.BlockSpec(memory_space=pltpu.VMEM)] * n,
        out_specs=pl.BlockSpec(memory_space=pl.ANY),
        out_shape=jax.ShapeDtypeStruct(shape, pieces[0].dtype),
        scratch_shapes=[pltpu.SemaphoreType.DMA((n,))],
        compiler_params=pltpu.CompilerParams(vmem_limit_bytes=2 * MIB),
        name="place",
    )(*pieces)


def local(queries, prefix_keys, prefix_values, suffix_keys, suffix_values, new_keys, new_values, suffix_lengths, out_weight):
    requests = queries.shape[0]
    even = lambda a: lax.ppermute(a, "z", E_PAIRS)
    odd = lambda a: lax.ppermute(a, "z", O_PAIRS)
    x1 = lambda a: lax.ppermute(a, "x", [(i, i ^ 1) for i in range(4)])
    x3 = lambda a: lax.ppermute(a, "x", [(i, i ^ 3) for i in range(4)])
    y = lambda a: lax.ppermute(a, "ylo", [(0, 1), (1, 0)])
    swap_core = lambda a: lax.ppermute(a, "core", [(0, 1), (1, 0)])
    swap_y = lambda a: lax.ppermute(a, "yhi", [(0, 1), (1, 0)])

    flat = lambda a: a.reshape(-1, a.shape[-1])
    args = [queries] + [flat(a) for a in (suffix_keys, suffix_values, new_keys, new_values)]
    after = lambda a, b: lax.optimization_barrier((a, b))[0]

    own = glue(pack_body, prefix_keys.shape[0], 2_000_000_000, prefix_keys, prefix_values)
    pair = glue(join_body, 2 * own.shape[0], 10_000_000_000, own, even(prefix_keys), even(prefix_values))
    r2 = odd(pair)
    q, m, acc = suffix(*args, suffix_lengths, r2)
    r3 = after(even(r2), m)
    r4 = odd(r3)
    line = jnp.concatenate([pair, r2, r3, r4], axis=0)
    b_x1, b_x3, b_y = x1(line), x3(line), y(line)
    m, acc = prefix(q, m, acc, [line])
    sent_y = after(b_y, m)
    b_yx1, b_yx3 = x1(sent_y), x3(sent_y)
    m, acc = prefix(q, m, acc, [b_y, b_x1])
    b_far, b_yfar = x1(after(b_x3, (b_yx1, m))), x3(after(b_yx1, m))
    m, acc = prefix(q, m, acc, [b_x3, b_yx1, b_yx3])

    shape = (requests, STEPS, out_weight.shape[1])
    cuts = (0, 16, 32, 48, 56, requests)
    low = cuts[1]
    mine, other_head, other_tail = final(q, m, acc, [b_far, b_yfar], out_weight, low)
    combine = lambda mine, got: (mine + got.astype(jnp.float32)).astype(jnp.bfloat16)
    head = combine(mine[:low], swap_core(other_head))
    tail = combine(mine[low:], swap_core(other_tail))
    pieces = [head] + [tail[a - low : b - low] for a, b in zip(cuts[1:], cuts[2:])]
    moved = [swap_y(piece) for piece in pieces]
    moved[:3] = lax.optimization_barrier(moved[:3])
    halves = []
    for piece, got in zip(pieces, moved):
        total = piece + got
        halves += [total, swap_core(total)]
    return place(halves, cuts[:-1], shape)


def solution(mesh):
    fine = Mesh(mesh.devices.reshape(2, 4, 8, 2, 2), ("ylo", "x", "z", "yhi", "core"))
    req, tp = ("ylo", "x", "z"), ("yhi", "core")
    in_specs = (
        P(req, None, tp),
        P(req, tp),
        P(req, tp),
        P(req, None, tp),
        P(req, None, tp),
        P(req, None, tp),
        P(req, None, tp),
        P(req),
        P(tp, None),
    )
    return jax.shard_map(local, mesh=fine, in_specs=in_specs, out_specs=P(req, None, None), check_vma=False)
```

```python
import math

import jax
import jax.numpy as jnp
from jax import lax
from jax.experimental import pallas as pl
from jax.experimental.pallas import tpu as pltpu
from jax.sharding import Mesh, PartitionSpec as P

HD = 128
GROUP = 8
STEPS = 4
SLOTS = 64
TOK = 16
PACK = TOK * GROUP
SCALE = math.log2(math.e) / math.sqrt(HD)
LOW = -1e30
MIB = 1024 * 1024

E_PAIRS = [(i, i ^ 1) for i in range(8)]
O_PAIRS = [(i, (i + 1) % 8 if i % 2 else (i - 1) % 8) for i in range(8)]
SKIP_PAIRS = [((i + 2) % 8 if i % 2 else (i - 2) % 8, i) for i in range(8)]


def dot_t(a, b):
    return lax.dot_general(a, b, (((1,), (1,)), ((), ())), preferred_element_type=jnp.float32)


def dot(a, b):
    return jnp.dot(a, b, preferred_element_type=jnp.float32)


def with_ones(v):
    return jnp.concatenate([v, jnp.ones_like(v)], axis=1)


def wide(a, count):
    return jnp.concatenate([a] * count, axis=1) if count > 1 else a


def row_max(s):
    top = s[:, :HD]
    for j in range(HD, s.shape[1], HD):
        top = jnp.maximum(top, s[:, j : j + HD])
    return jnp.max(top, axis=1, keepdims=True)


def pack_body(k_ref, v_ref, out_ref):
    out_ref[:, :HD] = k_ref[...]
    out_ref[:, HD:] = v_ref[...]


def join_body(own_ref, k_ref, v_ref, out_ref):
    rows = k_ref.shape[0]
    out_ref[:rows, :] = own_ref[...]
    out_ref[rows:, :HD] = k_ref[...]
    out_ref[rows:, HD:] = v_ref[...]


def glue(body, rows, flops, *arrays):
    return pl.pallas_call(
        body,
        out_shape=jax.ShapeDtypeStruct((rows, 2 * HD), arrays[0].dtype),
        cost_estimate=pl.CostEstimate(flops=flops, bytes_accessed=200_000, transcendentals=0),
        compiler_params=pltpu.CompilerParams(vmem_limit_bytes=MIB),
        name="glue",
    )(*arrays)


def suffix_body(q_ref, nk_ref, nv_ref, sk_all, sv_all, len_ref, _, qp_ref, m_ref, acc_ref, sk_held, sv_held, sem):
    packs = q_ref.shape[0] * STEPS // TOK
    base = pl.program_id(0) * packs
    per = TOK // STEPS
    keys = per * SLOTS
    now = pl.program_id(0)
    block = packs * keys

    def fetch(i):
        rows = pl.ds(pl.multiple_of(i * block, block), block)
        return [
            pltpu.make_async_copy(sk_all.at[rows, :], sk_held.at[i], sem.at[0, i]),
            pltpu.make_async_copy(sv_all.at[rows, :], sv_held.at[i], sem.at[1, i]),
        ]

    @pl.when(now == 0)
    def _():
        for i in range(sk_held.shape[0]):
            for copy in fetch(i):
                copy.start()

    for copy in fetch(now):
        copy.wait()
    sk_ref, sv_ref = sk_held.at[now], sv_held.at[now]
    row = lax.broadcasted_iota(jnp.int32, (PACK, keys), 0)
    col = lax.broadcasted_iota(jnp.int32, (PACK, keys), 1)
    owner = (row >> 2) & 3
    same = owner == (col >> 6)
    slot = col & (SLOTS - 1)
    row_n = lax.broadcasted_iota(jnp.int32, (PACK, TOK), 0)
    col_n = lax.broadcasted_iota(jnp.int32, (PACK, TOK), 1)
    same_n = (((row_n >> 2) & 3) == (col_n >> 2)) & ((col_n & 3) <= (row_n & 3))

    def scores(g):
        block = q_ref[g * per : (g + 1) * per, :, :].astype(jnp.float32)
        block = block.reshape(TOK, GROUP * HD).astype(jnp.bfloat16)
        q = jnp.concatenate([block[:, h * HD : (h + 1) * HD] for h in range(GROUP)], axis=0)
        qp_ref[g * PACK : (g + 1) * PACK, :] = q
        return dot_t(q, sk_ref[g * keys : (g + 1) * keys, :]), dot_t(q, nk_ref[g * TOK : (g + 1) * TOK, :])

    ahead = scores(0)
    for g in range(packs):
        s, s_n = ahead
        if g + 1 < packs:
            ahead = scores(g + 1)
        rows = pl.ds(g * PACK, PACK)
        length = jnp.full((PACK, keys), len_ref[(base + g) * per], jnp.int32)
        for j in range(1, per):
            length = jnp.where(owner == j, len_ref[(base + g) * per + j], length)
        s = jnp.where(same & (slot < length), s * SCALE, LOW)
        s_n = jnp.where(same_n, s_n * SCALE, LOW)
        m = jnp.maximum(row_max(s), jnp.max(s_n, axis=1, keepdims=True))
        p = jnp.exp2(s - m).astype(jnp.bfloat16)
        p_n = jnp.exp2(s_n - m).astype(jnp.bfloat16)
        new_v = nv_ref[g * TOK : (g + 1) * TOK, :]
        m_ref[rows, :] = jnp.broadcast_to(m, (PACK, HD))
        acc_ref[rows, :] = dot(p, with_ones(sv_ref[g * keys : (g + 1) * keys, :])) + dot(p_n, with_ones(new_v))


def suffix(q, sk, sv, nk, nv, lengths, after):
    rows = q.shape[0] * STEPS * GROUP
    grid = 4
    part = lambda a: pl.BlockSpec((a.shape[0] // grid,) + a.shape[1:], lambda i: (i,) + (0,) * (len(a.shape) - 1))
    outs = [
        jax.ShapeDtypeStruct((rows, HD), jnp.bfloat16),
        jax.ShapeDtypeStruct((rows, HD), jnp.float32),
        jax.ShapeDtypeStruct((rows, 2 * HD), jnp.float32),
    ]
    return pl.pallas_call(
        suffix_body,
        grid=(grid,),
        in_specs=[part(a) for a in (q, nk, nv)]
        + [pl.BlockSpec(memory_space=pltpu.HBM)] * 2
        + [pl.BlockSpec(memory_space=pltpu.SMEM), pl.BlockSpec(memory_space=pl.ANY)],
        out_specs=[part(o) for o in outs],
        out_shape=outs,
        scratch_shapes=[pltpu.VMEM((grid, sk.shape[0] // grid, HD), jnp.bfloat16)] * 2 + [pltpu.SemaphoreType.DMA((2, grid))],
        cost_estimate=pl.CostEstimate(flops=4_000_000_000, bytes_accessed=6_000_000, transcendentals=600_000),
        compiler_params=pltpu.CompilerParams(vmem_limit_bytes=12 * MIB),
        name="suffix",
    )(q, nk, nv, sk, sv, lengths, after)


def attend(q, m, acc, kvs, emit, tile=256):
    tiles = q.shape[0] // tile
    scores = lambda i: [dot_t(q[i * tile : (i + 1) * tile, :], kv[:, :HD]) for kv in kvs]
    ahead = scores(0)
    for i in range(tiles):
        parts = ahead
        if i + 1 < tiles:
            ahead = scores(i + 1)
        rows = slice(i * tile, (i + 1) * tile)
        top = row_max(parts[0])
        for s in parts[1:]:
            top = jnp.maximum(top, row_max(s))
        old = m[rows, :]
        new = jnp.maximum(old, top * SCALE)
        out = acc[rows, :] * wide(jnp.exp2(old - new), 2)
        for s, kv in zip(parts, kvs):
            p = jnp.exp2(s * SCALE - wide(new, s.shape[1] // HD)).astype(jnp.bfloat16)
            out = out + dot(p, with_ones(kv[:, HD:]))
        emit(i, rows, new, out)


def prefix_body(n, *refs):
    m_out, acc_out = refs[3 + n :]

    def emit(_, rows, new, out):
        m_out[rows, :] = new
        acc_out[rows, :] = out

    attend(refs[0], refs[1], refs[2], refs[3 : 3 + n], emit)


def prefix(q, m, acc, kvs, tile=1024):
    rows = q.shape[0]
    part = lambda a: pl.BlockSpec((tile, a.shape[1]), lambda i: (i, 0))
    whole = lambda a: pl.BlockSpec(a.shape, lambda i: (0, 0))
    keys = sum(kv.shape[0] for kv in kvs)
    return pl.pallas_call(
        lambda *refs: prefix_body(len(kvs), *refs),
        grid=(rows // tile,),
        in_specs=[part(q), part(m), part(acc)] + [whole(kv) for kv in kvs],
        out_specs=[part(m), part(acc)],
        out_shape=[jax.ShapeDtypeStruct(m.shape, m.dtype), jax.ShapeDtypeStruct(acc.shape, acc.dtype)],
        cost_estimate=pl.CostEstimate(flops=rows * keys * HD * 8, bytes_accessed=7_000_000, transcendentals=rows * keys),
        compiler_params=pltpu.CompilerParams(vmem_limit_bytes=16 * MIB),
        name="prefix",
    )(q, m, acc, *kvs)


def final_body(n, *refs):
    weight_ref, mine_ref, other_ref, heads_ref = refs[3 + n :]

    def emit(i, rows, _, out):
        heads = (out[:, :HD] / out[:, HD:]).astype(jnp.bfloat16)
        packs = heads.shape[0] // PACK
        for g in range(packs):
            for h in range(GROUP):
                first = g * PACK + h * TOK
                to = (i * packs + g) * TOK
                heads_ref[to : to + TOK, h * HD : (h + 1) * HD] = heads[first : first + TOK, :]

    attend(refs[0], refs[1], refs[2], refs[3 : 3 + n], emit)
    heads = heads_ref[...]
    requests, steps, half = mine_ref.shape
    core = lax.axis_index("core")
    width = 512
    for ref, side in ((other_ref, 1 - core), (mine_ref, core)):
        for j in range(0, half, width):
            columns = pl.ds(pl.multiple_of(side * half + j, width), width)
            terms = dot(heads, weight_ref[:, columns])
            ref[:, :, j : j + width] = terms.reshape(requests, steps, width).astype(ref.dtype)


def final(q, m, acc, kvs, weight, part, parts):
    rows = q.shape[0] // parts
    tokens, half = rows // GROUP, weight.shape[1] // 2
    keys = sum(kv.shape[0] for kv in kvs)
    whole = lambda a: pl.BlockSpec(a.shape, lambda i: (0,) * len(a.shape))
    shape = (tokens // STEPS, STEPS, half)
    outs = [jax.ShapeDtypeStruct(shape, jnp.float32), jax.ShapeDtypeStruct(shape, jnp.bfloat16)]
    return pl.pallas_call(
        lambda *refs: final_body(len(kvs), *refs),
        grid=(1,),
        in_specs=[pl.BlockSpec((rows, a.shape[1]), lambda i: (part, 0)) for a in (q, m, acc)]
        + [whole(kv) for kv in kvs]
        + [pl.BlockSpec(memory_space=pltpu.VMEM)],
        out_specs=[whole(o) for o in outs],
        out_shape=outs,
        scratch_shapes=[pltpu.VMEM((tokens, GROUP * HD), jnp.bfloat16)],
        cost_estimate=pl.CostEstimate(
            flops=rows * keys * HD * 8 + 8 * tokens * weight.size, bytes_accessed=12_000_000, transcendentals=rows * keys
        ),
        compiler_params=pltpu.CompilerParams(vmem_limit_bytes=24 * MIB),
        name="final",
    )(q, m, acc, *kvs, weight)


def place_body(n, lows, *refs):
    out_ref, sem = refs[-2:]
    half = refs[0].shape[2]
    core = lax.axis_index("core")
    copies = []
    for i in range(n):
        side = core if i % 2 == 0 else 1 - core
        rows = pl.ds(lows[i // 2], refs[i].shape[0])
        columns = pl.ds(pl.multiple_of(side * half, half), half)
        copies.append(pltpu.make_async_copy(refs[i], out_ref.at[rows, :, columns], sem.at[i]))
    for copy in copies:
        copy.start()
    for copy in copies:
        copy.wait()


def place(pieces, lows, shape):
    n = len(pieces)
    return pl.pallas_call(
        lambda *refs: place_body(n, lows, *refs),
        in_specs=[pl.BlockSpec(memory_space=pltpu.VMEM)] * n,
        out_specs=pl.BlockSpec(memory_space=pl.ANY),
        out_shape=jax.ShapeDtypeStruct(shape, pieces[0].dtype),
        scratch_shapes=[pltpu.SemaphoreType.DMA((n,))],
        compiler_params=pltpu.CompilerParams(vmem_limit_bytes=2 * MIB),
        name="place",
    )(*pieces)


def local(queries, prefix_keys, prefix_values, suffix_keys, suffix_values, new_keys, new_values, suffix_lengths, out_weight):
    requests = queries.shape[0]
    even = lambda a: lax.ppermute(a, "z", E_PAIRS)
    skip = lambda a: lax.ppermute(a, "z", SKIP_PAIRS)
    odd = lambda a: lax.ppermute(a, "z", O_PAIRS)
    x1 = lambda a: lax.ppermute(a, "x", [(i, i ^ 1) for i in range(4)])
    x3 = lambda a: lax.ppermute(a, "x", [(i, i ^ 3) for i in range(4)])
    y = lambda a: lax.ppermute(a, "ylo", [(0, 1), (1, 0)])
    swap_core = lambda a: lax.ppermute(a, "core", [(0, 1), (1, 0)])
    swap_y = lambda a: lax.ppermute(a, "yhi", [(0, 1), (1, 0)])

    flat = lambda a: a.reshape(-1, a.shape[-1])
    args = [queries] + [flat(a) for a in (suffix_keys, suffix_values, new_keys, new_values)]
    after = lambda a, b: lax.optimization_barrier((a, b))[0]

    own = glue(pack_body, prefix_keys.shape[0], 2_000_000_000, prefix_keys, prefix_values)
    pair = glue(join_body, 2 * own.shape[0], 10_000_000_000, own, even(prefix_keys), even(prefix_values))
    r2 = odd(pair)
    q, m, acc = suffix(*args, suffix_lengths, r2)
    r3, r4 = even(r2), after(skip(r2), m)
    line = jnp.concatenate([pair, r2, r3, r4], axis=0)
    b_x1, b_x3, b_y = x1(line), x3(line), y(line)
    m, acc = prefix(q, m, acc, [line])
    sent_y = after(b_y, m)
    b_yx1, b_yx3 = x1(sent_y), x3(sent_y)
    m, acc = prefix(q, m, acc, [b_y, b_x1])
    b_far, b_yfar = x1(after(b_x3, (b_yx1, m))), x3(after(b_yx1, m))
    m, acc = prefix(q, m, acc, [b_x3, b_yx1, b_yx3])

    shape = (requests, STEPS, out_weight.shape[1])
    last = [b_far, b_yfar]
    mine, other = final(q, m, acc, last, out_weight, 0, 2)
    mine_b, other_b = final(q, m, acc, last, out_weight, 1, 2)
    got = after(swap_core(other), mine_b)
    combine = lambda mine, got: (mine + got.astype(jnp.float32)).astype(jnp.bfloat16)
    cut = lambda a, sizes: [a[sum(sizes[:i]) : sum(sizes[: i + 1])] for i in range(len(sizes))]
    pieces = cut(combine(mine, got), (16, 16))
    pieces += cut(combine(mine_b, swap_core(other_b)), (16, 8, 8))
    moved = [swap_y(piece) for piece in pieces]
    moved[:3] = lax.optimization_barrier(moved[:3])
    halves, lows = [], [0]
    for piece, got in zip(pieces, moved):
        total = piece + got
        halves += [total, swap_core(total)]
        lows.append(lows[-1] + piece.shape[0])
    return place(halves, lows[:-1], shape)


def solution(mesh):
    fine = Mesh(mesh.devices.reshape(2, 4, 8, 2, 2), ("ylo", "x", "z", "yhi", "core"))
    req, tp = ("ylo", "x", "z"), ("yhi", "core")
    in_specs = (
        P(req, None, tp),
        P(req, tp),
        P(req, tp),
        P(req, None, tp),
        P(req, None, tp),
        P(req, None, tp),
        P(req, None, tp),
        P(req),
        P(tp, None),
    )
    return jax.shard_map(local, mesh=fine, in_specs=in_specs, out_specs=P(req, None, None), check_vma=False)
```

```python
import math

import jax
import jax.numpy as jnp
from jax import lax
from jax.experimental import pallas as pl
from jax.experimental.pallas import tpu as pltpu
from jax.sharding import Mesh, PartitionSpec as P

HD = 128
GROUP = 8
STEPS = 4
SLOTS = 64
TOK = 16
PACK = TOK * GROUP
SCALE = math.log2(math.e) / math.sqrt(HD)
LOW = -1e30
MIB = 1024 * 1024

E_PAIRS = [(i, i ^ 1) for i in range(8)]
O_PAIRS = [(i, (i + 1) % 8 if i % 2 else (i - 1) % 8) for i in range(8)]
SKIP_PAIRS = [((i + 2) % 8 if i % 2 else (i - 2) % 8, i) for i in range(8)]


def dot_t(a, b):
    return lax.dot_general(a, b, (((1,), (1,)), ((), ())), preferred_element_type=jnp.float32)


def dot(a, b):
    return jnp.dot(a, b, preferred_element_type=jnp.float32)


def with_ones(v):
    return jnp.concatenate([v, jnp.ones_like(v)], axis=1)


def wide(a, count):
    return jnp.concatenate([a] * count, axis=1) if count > 1 else a


def row_max(s):
    top = s[:, :HD]
    for j in range(HD, s.shape[1], HD):
        top = jnp.maximum(top, s[:, j : j + HD])
    return jnp.max(top, axis=1, keepdims=True)


def pack_body(k_ref, v_ref, out_ref):
    out_ref[:, :HD] = k_ref[...]
    out_ref[:, HD:] = v_ref[...]


def join_body(own_ref, k_ref, v_ref, out_ref):
    rows = k_ref.shape[0]
    out_ref[:rows, :] = own_ref[...]
    out_ref[rows:, :HD] = k_ref[...]
    out_ref[rows:, HD:] = v_ref[...]


def glue(body, rows, flops, *arrays):
    return pl.pallas_call(
        body,
        out_shape=jax.ShapeDtypeStruct((rows, 2 * HD), arrays[0].dtype),
        cost_estimate=pl.CostEstimate(flops=flops, bytes_accessed=200_000, transcendentals=0),
        compiler_params=pltpu.CompilerParams(vmem_limit_bytes=MIB),
        name="glue",
    )(*arrays)


def suffix_body(first, q_ref, nk_ref, nv_ref, sk_all, sv_all, len_ref, *refs):
    qp_ref, m_ref, acc_ref, sk_held, sv_held, sem = refs[-6:]
    packs = q_ref.shape[0] * STEPS // TOK
    base = (first + pl.program_id(0)) * packs
    per = TOK // STEPS
    keys = per * SLOTS
    now = pl.program_id(0)
    block = packs * keys

    def fetch(i):
        rows = pl.ds(pl.multiple_of((first + i) * block, block), block)
        return [
            pltpu.make_async_copy(sk_all.at[rows, :], sk_held.at[i], sem.at[0, i]),
            pltpu.make_async_copy(sv_all.at[rows, :], sv_held.at[i], sem.at[1, i]),
        ]

    @pl.when(now == 0)
    def _():
        for i in range(sk_held.shape[0]):
            for copy in fetch(i):
                copy.start()

    for copy in fetch(now):
        copy.wait()
    sk_ref, sv_ref = sk_held.at[now], sv_held.at[now]
    row = lax.broadcasted_iota(jnp.int32, (PACK, keys), 0)
    col = lax.broadcasted_iota(jnp.int32, (PACK, keys), 1)
    owner = (row >> 2) & 3
    same = owner == (col >> 6)
    slot = col & (SLOTS - 1)
    row_n = lax.broadcasted_iota(jnp.int32, (PACK, TOK), 0)
    col_n = lax.broadcasted_iota(jnp.int32, (PACK, TOK), 1)
    same_n = (((row_n >> 2) & 3) == (col_n >> 2)) & ((col_n & 3) <= (row_n & 3))

    def scores(g):
        block = q_ref[g * per : (g + 1) * per, :, :].astype(jnp.float32)
        block = block.reshape(TOK, GROUP * HD).astype(jnp.bfloat16)
        q = jnp.concatenate([block[:, h * HD : (h + 1) * HD] for h in range(GROUP)], axis=0)
        qp_ref[g * PACK : (g + 1) * PACK, :] = q
        return dot_t(q, sk_ref[g * keys : (g + 1) * keys, :]), dot_t(q, nk_ref[g * TOK : (g + 1) * TOK, :])

    ahead = scores(0)
    for g in range(packs):
        s, s_n = ahead
        if g + 1 < packs:
            ahead = scores(g + 1)
        rows = pl.ds(g * PACK, PACK)
        length = jnp.full((PACK, keys), len_ref[(base + g) * per], jnp.int32)
        for j in range(1, per):
            length = jnp.where(owner == j, len_ref[(base + g) * per + j], length)
        s = jnp.where(same & (slot < length), s * SCALE, LOW)
        s_n = jnp.where(same_n, s_n * SCALE, LOW)
        m = jnp.maximum(row_max(s), jnp.max(s_n, axis=1, keepdims=True))
        p = jnp.exp2(s - m).astype(jnp.bfloat16)
        p_n = jnp.exp2(s_n - m).astype(jnp.bfloat16)
        new_v = nv_ref[g * TOK : (g + 1) * TOK, :]
        m_ref[rows, :] = jnp.broadcast_to(m, (PACK, HD))
        acc_ref[rows, :] = dot(p, with_ones(sv_ref[g * keys : (g + 1) * keys, :])) + dot(p_n, with_ones(new_v))


def suffix(q, sk, sv, nk, nv, lengths, later, half, state=()):
    rows = q.shape[0] * STEPS * GROUP
    grid = 2
    first = half * grid
    part = lambda a: pl.BlockSpec((a.shape[0] // (2 * grid),) + a.shape[1:], lambda i: (first + i,) + (0,) * (len(a.shape) - 1))
    outs = [
        jax.ShapeDtypeStruct((rows, HD), jnp.bfloat16),
        jax.ShapeDtypeStruct((rows, HD), jnp.float32),
        jax.ShapeDtypeStruct((rows, 2 * HD), jnp.float32),
    ]
    return pl.pallas_call(
        lambda *refs: suffix_body(first, *refs),
        grid=(grid,),
        in_specs=[part(a) for a in (q, nk, nv)]
        + [pl.BlockSpec(memory_space=pltpu.HBM)] * 2
        + [pl.BlockSpec(memory_space=pltpu.SMEM)]
        + [pl.BlockSpec(memory_space=pl.ANY)] * (1 + len(state)),
        out_specs=[part(o) for o in outs],
        out_shape=outs,
        input_output_aliases={7 + i: i for i in range(len(state))},
        scratch_shapes=[pltpu.VMEM((grid, sk.shape[0] // (2 * grid), HD), jnp.bfloat16)] * 2 + [pltpu.SemaphoreType.DMA((2, grid))],
        cost_estimate=pl.CostEstimate(flops=2_000_000_000, bytes_accessed=3_000_000, transcendentals=300_000),
        compiler_params=pltpu.CompilerParams(vmem_limit_bytes=12 * MIB),
        name="suffix",
    )(q, nk, nv, sk, sv, lengths, later, *state)


def attend(q, m, acc, kvs, emit, tile=512):
    tiles = q.shape[0] // tile
    scores = lambda i: [dot_t(q[i * tile : (i + 1) * tile, :], kv[:, :HD]) for kv in kvs]
    ahead = scores(0)
    for i in range(tiles):
        parts = ahead
        if i + 1 < tiles:
            ahead = scores(i + 1)
        rows = slice(i * tile, (i + 1) * tile)
        top = row_max(parts[0])
        for s in parts[1:]:
            top = jnp.maximum(top, row_max(s))
        old = m[rows, :]
        new = jnp.maximum(old, top * SCALE)
        out = acc[rows, :] * wide(jnp.exp2(old - new), 2)
        for s, kv in zip(parts, kvs):
            p = jnp.exp2(s * SCALE - wide(new, s.shape[1] // HD)).astype(jnp.bfloat16)
            out = out + dot(p, with_ones(kv[:, HD:]))
        emit(i, rows, new, out)


def prefix_body(n, *refs):
    m_out, acc_out = refs[3 + n :]

    def emit(_, rows, new, out):
        m_out[rows, :] = new
        acc_out[rows, :] = out

    attend(refs[0], refs[1], refs[2], refs[3 : 3 + n], emit)


def prefix(q, m, acc, kvs, tile=1024):
    rows = q.shape[0]
    part = lambda a: pl.BlockSpec((tile, a.shape[1]), lambda i: (i, 0))
    whole = lambda a: pl.BlockSpec(a.shape, lambda i: (0, 0))
    keys = sum(kv.shape[0] for kv in kvs)
    return pl.pallas_call(
        lambda *refs: prefix_body(len(kvs), *refs),
        grid=(rows // tile,),
        in_specs=[part(q), part(m), part(acc)] + [whole(kv) for kv in kvs],
        out_specs=[part(m), part(acc)],
        out_shape=[jax.ShapeDtypeStruct(m.shape, m.dtype), jax.ShapeDtypeStruct(acc.shape, acc.dtype)],
        cost_estimate=pl.CostEstimate(flops=rows * keys * HD * 8, bytes_accessed=7_000_000, transcendentals=rows * keys),
        compiler_params=pltpu.CompilerParams(vmem_limit_bytes=24 * MIB),
        name="prefix",
    )(q, m, acc, *kvs)


def final_body(n, *refs):
    weight_ref, mine_ref, other_ref, heads_ref = refs[3 + n :]

    def emit(i, rows, _, out):
        heads = (out[:, :HD] / out[:, HD:]).astype(jnp.bfloat16)
        packs = heads.shape[0] // PACK
        for g in range(packs):
            for h in range(GROUP):
                first = g * PACK + h * TOK
                to = (i * packs + g) * TOK
                heads_ref[to : to + TOK, h * HD : (h + 1) * HD] = heads[first : first + TOK, :]

    attend(refs[0], refs[1], refs[2], refs[3 : 3 + n], emit)
    heads = heads_ref[...]
    requests, steps, half = mine_ref.shape
    core = lax.axis_index("core")
    width = 512
    for ref, side in ((other_ref, 1 - core), (mine_ref, core)):
        for j in range(0, half, width):
            columns = pl.ds(pl.multiple_of(side * half + j, width), width)
            terms = dot(heads, weight_ref[:, columns])
            ref[:, :, j : j + width] = terms.reshape(requests, steps, width).astype(ref.dtype)


def final(q, m, acc, kvs, weight, part, parts):
    rows = q.shape[0] // parts
    tokens, half = rows // GROUP, weight.shape[1] // 2
    keys = sum(kv.shape[0] for kv in kvs)
    whole = lambda a: pl.BlockSpec(a.shape, lambda i: (0,) * len(a.shape))
    shape = (tokens // STEPS, STEPS, half)
    outs = [jax.ShapeDtypeStruct(shape, jnp.float32), jax.ShapeDtypeStruct(shape, jnp.bfloat16)]
    return pl.pallas_call(
        lambda *refs: final_body(len(kvs), *refs),
        grid=(1,),
        in_specs=[pl.BlockSpec((rows, a.shape[1]), lambda i: (part, 0)) for a in (q, m, acc)]
        + [whole(kv) for kv in kvs]
        + [pl.BlockSpec(memory_space=pltpu.VMEM)],
        out_specs=[whole(o) for o in outs],
        out_shape=outs,
        scratch_shapes=[pltpu.VMEM((tokens, GROUP * HD), jnp.bfloat16)],
        cost_estimate=pl.CostEstimate(
            flops=rows * keys * HD * 8 + 8 * tokens * weight.size, bytes_accessed=12_000_000, transcendentals=rows * keys
        ),
        compiler_params=pltpu.CompilerParams(vmem_limit_bytes=24 * MIB),
        name="final",
    )(q, m, acc, *kvs, weight)


def place_body(n, lows, *refs):
    out_ref, sem = refs[-2:]
    half = refs[0].shape[2]
    core = lax.axis_index("core")
    copies = []
    for i in range(n):
        side = core if i % 2 == 0 else 1 - core
        rows = pl.ds(lows[i // 2], refs[i].shape[0])
        columns = pl.ds(pl.multiple_of(side * half, half), half)
        copies.append(pltpu.make_async_copy(refs[i], out_ref.at[rows, :, columns], sem.at[i]))
    for copy in copies:
        copy.start()
    for copy in copies:
        copy.wait()


def place(pieces, lows, shape):
    n = len(pieces)
    return pl.pallas_call(
        lambda *refs: place_body(n, lows, *refs),
        in_specs=[pl.BlockSpec(memory_space=pltpu.VMEM)] * n,
        out_specs=pl.BlockSpec(memory_space=pl.ANY),
        out_shape=jax.ShapeDtypeStruct(shape, pieces[0].dtype),
        scratch_shapes=[pltpu.SemaphoreType.DMA((n,))],
        compiler_params=pltpu.CompilerParams(vmem_limit_bytes=2 * MIB),
        name="place",
    )(*pieces)


def local(queries, prefix_keys, prefix_values, suffix_keys, suffix_values, new_keys, new_values, suffix_lengths, out_weight):
    requests = queries.shape[0]
    even = lambda a: lax.ppermute(a, "z", E_PAIRS)
    skip = lambda a: lax.ppermute(a, "z", SKIP_PAIRS)
    odd = lambda a: lax.ppermute(a, "z", O_PAIRS)
    x1 = lambda a: lax.ppermute(a, "x", [(i, i ^ 1) for i in range(4)])
    x3 = lambda a: lax.ppermute(a, "x", [(i, i ^ 3) for i in range(4)])
    y = lambda a: lax.ppermute(a, "ylo", [(0, 1), (1, 0)])
    swap_core = lambda a: lax.ppermute(a, "core", [(0, 1), (1, 0)])
    swap_y = lambda a: lax.ppermute(a, "yhi", [(0, 1), (1, 0)])

    flat = lambda a: a.reshape(-1, a.shape[-1])
    args = [queries] + [flat(a) for a in (suffix_keys, suffix_values, new_keys, new_values)]
    after = lambda a, b: lax.optimization_barrier((a, b))[0]

    own = glue(pack_body, prefix_keys.shape[0], 2_000_000_000, prefix_keys, prefix_values)
    pair = glue(join_body, 2 * own.shape[0], 10_000_000_000, own, even(prefix_keys), even(prefix_values))
    state = suffix(*args, suffix_lengths, pair, 0)
    r2 = after(odd(pair), state[1])
    q, m, acc = suffix(*args, suffix_lengths, r2, 1, state)
    r3, r4 = even(r2), after(skip(r2), m)
    line = jnp.concatenate([pair, r2, r3, r4], axis=0)
    b_x1, b_x3, b_y = x1(line), x3(line), y(line)
    m, acc = prefix(q, m, acc, [line])
    sent_y = after(b_y, m)
    b_yx1, b_yx3 = x1(sent_y), x3(sent_y)
    m, acc = prefix(q, m, acc, [b_y, b_x1])
    b_far, b_yfar = x1(after(b_x3, (b_yx1, m))), x3(after(b_yx1, m))
    m, acc = prefix(q, m, acc, [b_x3, b_yx1, b_yx3])

    shape = (requests, STEPS, out_weight.shape[1])
    last = [b_far, b_yfar]
    mine, other = final(q, m, acc, last, out_weight, 0, 2)
    mine_b, other_b = final(q, m, acc, last, out_weight, 1, 2)
    got = after(swap_core(other), mine_b)
    combine = lambda mine, got: (mine + got.astype(jnp.float32)).astype(jnp.bfloat16)
    cut = lambda a, sizes: [a[sum(sizes[:i]) : sum(sizes[: i + 1])] for i in range(len(sizes))]
    low = requests // 4
    pieces = [combine(mine[:low], got[:low])]
    pieces += [combine(mine[low:], after(got, pieces[0])[low:])]
    pieces += cut(combine(mine_b, swap_core(other_b)), (16, 8, 8))
    moved = [swap_y(piece) for piece in pieces]
    moved[:3] = lax.optimization_barrier(moved[:3])
    halves, lows = [], [0]
    for piece, got in zip(pieces, moved):
        total = piece + got
        halves += [total, swap_core(total)]
        lows.append(lows[-1] + piece.shape[0])
    return place(halves, lows[:-1], shape)


def solution(mesh):
    fine = Mesh(mesh.devices.reshape(2, 4, 8, 2, 2), ("ylo", "x", "z", "yhi", "core"))
    req, tp = ("ylo", "x", "z"), ("yhi", "core")
    in_specs = (
        P(req, None, tp),
        P(req, tp),
        P(req, tp),
        P(req, None, tp),
        P(req, None, tp),
        P(req, None, tp),
        P(req, None, tp),
        P(req),
        P(tp, None),
    )
    return jax.shard_map(local, mesh=fine, in_specs=in_specs, out_specs=P(req, None, None), check_vma=False)
```

```python
import math

import jax
import jax.numpy as jnp
from jax import lax
from jax.experimental import pallas as pl
from jax.experimental.pallas import tpu as pltpu
from jax.sharding import Mesh, PartitionSpec as P

HD = 128
GROUP = 8
STEPS = 4
SLOTS = 64
TOK = 16
PACK = TOK * GROUP
SCALE = math.log2(math.e) / math.sqrt(HD)
LOW = -1e30
MIB = 1024 * 1024

E_PAIRS = [(i, i ^ 1) for i in range(8)]
O_PAIRS = [(i, (i + 1) % 8 if i % 2 else (i - 1) % 8) for i in range(8)]
SKIP_PAIRS = [(i, (i - 3) % 8 if i % 2 else (i + 3) % 8) for i in range(8)]


def dot_t(a, b):
    return lax.dot_general(a, b, (((1,), (1,)), ((), ())), preferred_element_type=jnp.float32)


def dot(a, b):
    return jnp.dot(a, b, preferred_element_type=jnp.float32)


def with_ones(v):
    return jnp.concatenate([v, jnp.ones_like(v)], axis=1)


def wide(a, count):
    return jnp.concatenate([a] * count, axis=1) if count > 1 else a


def row_max(s):
    top = s[:, :HD]
    for j in range(HD, s.shape[1], HD):
        top = jnp.maximum(top, s[:, j : j + HD])
    return jnp.max(top, axis=1, keepdims=True)


def pack_body(k_ref, v_ref, out_ref):
    out_ref[:, :HD] = k_ref[...]
    out_ref[:, HD:] = v_ref[...]


def join_body(own_ref, k_ref, v_ref, out_ref):
    rows = k_ref.shape[0]
    out_ref[:rows, :] = own_ref[...]
    out_ref[rows:, :HD] = k_ref[...]
    out_ref[rows:, HD:] = v_ref[...]


def glue(body, rows, flops, *arrays):
    return pl.pallas_call(
        body,
        out_shape=jax.ShapeDtypeStruct((rows, 2 * HD), arrays[0].dtype),
        cost_estimate=pl.CostEstimate(flops=flops, bytes_accessed=200_000, transcendentals=0),
        compiler_params=pltpu.CompilerParams(vmem_limit_bytes=MIB),
        name="glue",
    )(*arrays)


def suffix_body(first, q_ref, nk_ref, nv_ref, sk_all, sv_all, len_ref, *refs):
    qp_ref, m_ref, acc_ref, sk_held, sv_held, sem = refs[-6:]
    packs = q_ref.shape[0] * STEPS // TOK
    base = (first + pl.program_id(0)) * packs
    per = TOK // STEPS
    keys = per * SLOTS
    now = pl.program_id(0)
    block = packs * keys

    def fetch(i):
        rows = pl.ds(pl.multiple_of((first + i) * block, block), block)
        return [
            pltpu.make_async_copy(sk_all.at[rows, :], sk_held.at[i], sem.at[0, i]),
            pltpu.make_async_copy(sv_all.at[rows, :], sv_held.at[i], sem.at[1, i]),
        ]

    @pl.when(now == 0)
    def _():
        for i in range(sk_held.shape[0]):
            for copy in fetch(i):
                copy.start()

    for copy in fetch(now):
        copy.wait()
    sk_ref, sv_ref = sk_held.at[now], sv_held.at[now]
    row = lax.broadcasted_iota(jnp.int32, (PACK, keys), 0)
    col = lax.broadcasted_iota(jnp.int32, (PACK, keys), 1)
    owner = (row >> 2) & 3
    same = owner == (col >> 6)
    slot = col & (SLOTS - 1)
    row_n = lax.broadcasted_iota(jnp.int32, (PACK, TOK), 0)
    col_n = lax.broadcasted_iota(jnp.int32, (PACK, TOK), 1)
    same_n = (((row_n >> 2) & 3) == (col_n >> 2)) & ((col_n & 3) <= (row_n & 3))

    def scores(g):
        block = q_ref[g * per : (g + 1) * per, :, :].astype(jnp.float32)
        block = block.reshape(TOK, GROUP * HD).astype(jnp.bfloat16)
        q = jnp.concatenate([block[:, h * HD : (h + 1) * HD] for h in range(GROUP)], axis=0)
        qp_ref[g * PACK : (g + 1) * PACK, :] = q
        return dot_t(q, sk_ref[g * keys : (g + 1) * keys, :]), dot_t(q, nk_ref[g * TOK : (g + 1) * TOK, :])

    ahead = scores(0)
    for g in range(packs):
        s, s_n = ahead
        if g + 1 < packs:
            ahead = scores(g + 1)
        rows = pl.ds(g * PACK, PACK)
        length = jnp.full((PACK, keys), len_ref[(base + g) * per], jnp.int32)
        for j in range(1, per):
            length = jnp.where(owner == j, len_ref[(base + g) * per + j], length)
        s = jnp.where(same & (slot < length), s * SCALE, LOW)
        s_n = jnp.where(same_n, s_n * SCALE, LOW)
        m = jnp.maximum(row_max(s), jnp.max(s_n, axis=1, keepdims=True))
        p = jnp.exp2(s - m).astype(jnp.bfloat16)
        p_n = jnp.exp2(s_n - m).astype(jnp.bfloat16)
        new_v = nv_ref[g * TOK : (g + 1) * TOK, :]
        m_ref[rows, :] = jnp.broadcast_to(m, (PACK, HD))
        acc_ref[rows, :] = dot(p, with_ones(sv_ref[g * keys : (g + 1) * keys, :])) + dot(p_n, with_ones(new_v))


def suffix(q, sk, sv, nk, nv, lengths, later, half, state=()):
    rows = q.shape[0] * STEPS * GROUP
    grid = 2
    first = half * grid
    part = lambda a: pl.BlockSpec((a.shape[0] // (2 * grid),) + a.shape[1:], lambda i: (first + i,) + (0,) * (len(a.shape) - 1))
    outs = [
        jax.ShapeDtypeStruct((rows, HD), jnp.bfloat16),
        jax.ShapeDtypeStruct((rows, HD), jnp.float32),
        jax.ShapeDtypeStruct((rows, 2 * HD), jnp.float32),
    ]
    return pl.pallas_call(
        lambda *refs: suffix_body(first, *refs),
        grid=(grid,),
        in_specs=[part(a) for a in (q, nk, nv)]
        + [pl.BlockSpec(memory_space=pltpu.HBM)] * 2
        + [pl.BlockSpec(memory_space=pltpu.SMEM)]
        + [pl.BlockSpec(memory_space=pl.ANY)] * (1 + len(state)),
        out_specs=[part(o) for o in outs],
        out_shape=outs,
        input_output_aliases={7 + i: i for i in range(len(state))},
        scratch_shapes=[pltpu.VMEM((grid, sk.shape[0] // (2 * grid), HD), jnp.bfloat16)] * 2 + [pltpu.SemaphoreType.DMA((2, grid))],
        cost_estimate=pl.CostEstimate(flops=2_000_000_000, bytes_accessed=3_000_000, transcendentals=300_000),
        compiler_params=pltpu.CompilerParams(vmem_limit_bytes=12 * MIB),
        name="suffix",
    )(q, nk, nv, sk, sv, lengths, later, *state)


def attend(q, m, acc, kvs, emit, tile=512):
    tiles = q.shape[0] // tile
    scores = lambda i: [dot_t(q[i * tile : (i + 1) * tile, :], kv[:, :HD]) for kv in kvs]
    ahead = scores(0)
    for i in range(tiles):
        parts = ahead
        if i + 1 < tiles:
            ahead = scores(i + 1)
        rows = slice(i * tile, (i + 1) * tile)
        top = row_max(parts[0])
        for s in parts[1:]:
            top = jnp.maximum(top, row_max(s))
        old = m[rows, :]
        new = jnp.maximum(old, top * SCALE)
        out = acc[rows, :] * wide(jnp.exp2(old - new), 2)
        for s, kv in zip(parts, kvs):
            p = jnp.exp2(s * SCALE - wide(new, s.shape[1] // HD)).astype(jnp.bfloat16)
            out = out + dot(p, with_ones(kv[:, HD:]))
        emit(i, rows, new, out)


def prefix_body(n, *refs):
    m_out, acc_out = refs[3 + n :]

    def emit(_, rows, new, out):
        m_out[rows, :] = new
        acc_out[rows, :] = out

    attend(refs[0], refs[1], refs[2], refs[3 : 3 + n], emit)


def prefix(q, m, acc, kvs, tile=1024):
    rows = q.shape[0]
    part = lambda a: pl.BlockSpec((tile, a.shape[1]), lambda i: (i, 0))
    whole = lambda a: pl.BlockSpec(a.shape, lambda i: (0, 0))
    keys = sum(kv.shape[0] for kv in kvs)
    return pl.pallas_call(
        lambda *refs: prefix_body(len(kvs), *refs),
        grid=(rows // tile,),
        in_specs=[part(q), part(m), part(acc)] + [whole(kv) for kv in kvs],
        out_specs=[part(m), part(acc)],
        out_shape=[jax.ShapeDtypeStruct(m.shape, m.dtype), jax.ShapeDtypeStruct(acc.shape, acc.dtype)],
        cost_estimate=pl.CostEstimate(flops=rows * keys * HD * 8, bytes_accessed=7_000_000, transcendentals=rows * keys),
        compiler_params=pltpu.CompilerParams(vmem_limit_bytes=24 * MIB),
        name="prefix",
    )(q, m, acc, *kvs)


def final_body(n, *refs):
    weight_ref, mine_ref, other_ref, heads_ref = refs[3 + n :]

    def emit(i, rows, _, out):
        heads = (out[:, :HD] / out[:, HD:]).astype(jnp.bfloat16)
        packs = heads.shape[0] // PACK
        for g in range(packs):
            for h in range(GROUP):
                first = g * PACK + h * TOK
                to = (i * packs + g) * TOK
                heads_ref[to : to + TOK, h * HD : (h + 1) * HD] = heads[first : first + TOK, :]

    attend(refs[0], refs[1], refs[2], refs[3 : 3 + n], emit)
    heads = heads_ref[...]
    requests, steps, half = mine_ref.shape
    core = lax.axis_index("core")
    width = 512
    for ref, side in ((other_ref, 1 - core), (mine_ref, core)):
        for j in range(0, half, width):
            columns = pl.ds(pl.multiple_of(side * half + j, width), width)
            terms = dot(heads, weight_ref[:, columns])
            ref[:, :, j : j + width] = terms.reshape(requests, steps, width).astype(ref.dtype)


def final(q, m, acc, kvs, weight, part, parts):
    rows = q.shape[0] // parts
    tokens, half = rows // GROUP, weight.shape[1] // 2
    keys = sum(kv.shape[0] for kv in kvs)
    whole = lambda a: pl.BlockSpec(a.shape, lambda i: (0,) * len(a.shape))
    shape = (tokens // STEPS, STEPS, half)
    outs = [jax.ShapeDtypeStruct(shape, jnp.float32), jax.ShapeDtypeStruct(shape, jnp.bfloat16)]
    return pl.pallas_call(
        lambda *refs: final_body(len(kvs), *refs),
        grid=(1,),
        in_specs=[pl.BlockSpec((rows, a.shape[1]), lambda i: (part, 0)) for a in (q, m, acc)]
        + [whole(kv) for kv in kvs]
        + [pl.BlockSpec(memory_space=pltpu.VMEM)],
        out_specs=[whole(o) for o in outs],
        out_shape=outs,
        scratch_shapes=[pltpu.VMEM((tokens, GROUP * HD), jnp.bfloat16)],
        cost_estimate=pl.CostEstimate(
            flops=rows * keys * HD * 8 + 8 * tokens * weight.size, bytes_accessed=12_000_000, transcendentals=rows * keys
        ),
        compiler_params=pltpu.CompilerParams(vmem_limit_bytes=24 * MIB),
        name="final",
    )(q, m, acc, *kvs, weight)


def place_body(n, lows, *refs):
    out_ref, sem = refs[-2:]
    half = refs[0].shape[2]
    core = lax.axis_index("core")
    copies = []
    for i in range(n):
        side = core if i % 2 == 0 else 1 - core
        rows = pl.ds(lows[i // 2], refs[i].shape[0])
        columns = pl.ds(pl.multiple_of(side * half, half), half)
        copies.append(pltpu.make_async_copy(refs[i], out_ref.at[rows, :, columns], sem.at[i]))
    for copy in copies:
        copy.start()
    for copy in copies:
        copy.wait()


def place(pieces, lows, shape):
    n = len(pieces)
    return pl.pallas_call(
        lambda *refs: place_body(n, lows, *refs),
        in_specs=[pl.BlockSpec(memory_space=pltpu.VMEM)] * n,
        out_specs=pl.BlockSpec(memory_space=pl.ANY),
        out_shape=jax.ShapeDtypeStruct(shape, pieces[0].dtype),
        scratch_shapes=[pltpu.SemaphoreType.DMA((n,))],
        compiler_params=pltpu.CompilerParams(vmem_limit_bytes=2 * MIB),
        name="place",
    )(*pieces)


def local(queries, prefix_keys, prefix_values, suffix_keys, suffix_values, new_keys, new_values, suffix_lengths, out_weight):
    requests = queries.shape[0]
    even = lambda a: lax.ppermute(a, "z", E_PAIRS)
    skip = lambda a: lax.ppermute(a, "z", SKIP_PAIRS)
    odd = lambda a: lax.ppermute(a, "z", O_PAIRS)
    x1 = lambda a: lax.ppermute(a, "x", [(i, i ^ 1) for i in range(4)])
    x3 = lambda a: lax.ppermute(a, "x", [(i, i ^ 3) for i in range(4)])
    y = lambda a: lax.ppermute(a, "ylo", [(0, 1), (1, 0)])
    swap_core = lambda a: lax.ppermute(a, "core", [(0, 1), (1, 0)])
    swap_y = lambda a: lax.ppermute(a, "yhi", [(0, 1), (1, 0)])

    flat = lambda a: a.reshape(-1, a.shape[-1])
    args = [queries] + [flat(a) for a in (suffix_keys, suffix_values, new_keys, new_values)]
    after = lambda a, b: lax.optimization_barrier((a, b))[0]

    own = glue(pack_body, prefix_keys.shape[0], 2_000_000_000, prefix_keys, prefix_values)
    pair = glue(join_body, 2 * own.shape[0], 10_000_000_000, own, even(prefix_keys), even(prefix_values))
    state = suffix(*args, suffix_lengths, pair, 0)
    r2 = after(odd(pair), state[1])
    q, m, acc = suffix(*args, suffix_lengths, r2, 1, state)
    r3, r4 = even(r2), after(skip(r2), m)
    line = jnp.concatenate([pair, r2, r3, r4], axis=0)
    b_x1, b_x3, b_y = x1(line), x3(line), y(line)
    m, acc = prefix(q, m, acc, [line])
    sent_y = after(b_y, m)
    b_yx1, b_yx3 = x1(sent_y), x3(sent_y)
    m, acc = prefix(q, m, acc, [b_y, b_x1])
    b_far, b_yfar = x1(after(b_x3, (b_yx1, m))), x3(after(b_yx1, m))
    m, acc = prefix(q, m, acc, [b_x3, b_yx1, b_yx3])

    shape = (requests, STEPS, out_weight.shape[1])
    last = [b_far, b_yfar]
    mine, other = final(q, m, acc, last, out_weight, 0, 2)
    mine_b, other_b = final(q, m, acc, last, out_weight, 1, 2)
    got = after(swap_core(other), mine_b)
    combine = lambda mine, got: (mine + got.astype(jnp.float32)).astype(jnp.bfloat16)
    cut = lambda a, sizes: [a[sum(sizes[:i]) : sum(sizes[: i + 1])] for i in range(len(sizes))]
    low = requests // 4
    pieces = [combine(mine[:low], got[:low])]
    pieces += [combine(mine[low:], after(got, pieces[0])[low:])]
    pieces += cut(combine(mine_b, swap_core(after(other_b, pieces[0]))), (24, 8))
    moved = [swap_y(piece) for piece in pieces]
    moved[:3] = lax.optimization_barrier(moved[:3])
    halves, lows = [], [0]
    for piece, got in zip(pieces, moved):
        total = piece + got
        halves += [total, swap_core(total)]
        lows.append(lows[-1] + piece.shape[0])
    return place(halves, lows[:-1], shape)


def solution(mesh):
    fine = Mesh(mesh.devices.reshape(2, 4, 8, 2, 2), ("ylo", "x", "z", "yhi", "core"))
    req, tp = ("ylo", "x", "z"), ("yhi", "core")
    in_specs = (
        P(req, None, tp),
        P(req, tp),
        P(req, tp),
        P(req, None, tp),
        P(req, None, tp),
        P(req, None, tp),
        P(req, None, tp),
        P(req),
        P(tp, None),
    )
    return jax.shard_map(local, mesh=fine, in_specs=in_specs, out_specs=P(req, None, None), check_vma=False)
```

```python
import math

import jax
import jax.numpy as jnp
from jax import lax
from jax.experimental import pallas as pl
from jax.experimental.pallas import tpu as pltpu
from jax.sharding import Mesh, PartitionSpec as P

HD = 128
GROUP = 8
STEPS = 4
SLOTS = 64
TOK = 16
PACK = TOK * GROUP
SCALE = math.log2(math.e) / math.sqrt(HD)
LOW = -1e30
MIB = 1024 * 1024

E_PAIRS = [(i, i ^ 1) for i in range(8)]
O_PAIRS = [(i, (i + 1) % 8 if i % 2 else (i - 1) % 8) for i in range(8)]
SKIP_PAIRS = [(i, (i - 3) % 8 if i % 2 else (i + 3) % 8) for i in range(8)]


def dot_t(a, b):
    return lax.dot_general(a, b, (((1,), (1,)), ((), ())), preferred_element_type=jnp.float32)


def dot(a, b):
    return jnp.dot(a, b, preferred_element_type=jnp.float32)


def with_ones(v):
    return jnp.concatenate([v, jnp.ones_like(v)], axis=1)


def wide(a, count):
    return jnp.concatenate([a] * count, axis=1) if count > 1 else a


def row_max(s):
    top = s[:, :HD]
    for j in range(HD, s.shape[1], HD):
        top = jnp.maximum(top, s[:, j : j + HD])
    return jnp.max(top, axis=1, keepdims=True)


def pack_body(k_ref, v_ref, out_ref):
    out_ref[:, :HD] = k_ref[...]
    out_ref[:, HD:] = v_ref[...]


def join_body(own_ref, k_ref, v_ref, out_ref):
    rows = k_ref.shape[0]
    out_ref[:rows, :] = own_ref[...]
    out_ref[rows:, :HD] = k_ref[...]
    out_ref[rows:, HD:] = v_ref[...]


def glue(body, rows, flops, *arrays):
    return pl.pallas_call(
        body,
        out_shape=jax.ShapeDtypeStruct((rows, 2 * HD), arrays[0].dtype),
        cost_estimate=pl.CostEstimate(flops=flops, bytes_accessed=200_000, transcendentals=0),
        compiler_params=pltpu.CompilerParams(vmem_limit_bytes=MIB),
        name="glue",
    )(*arrays)


def suffix_body(first, q_ref, nk_ref, nv_ref, sk_all, sv_all, len_ref, *refs):
    qp_ref, m_ref, acc_ref, sk_held, sv_held, sem = refs[-6:]
    packs = q_ref.shape[0] * STEPS // TOK
    base = (first + pl.program_id(0)) * packs
    per = TOK // STEPS
    keys = per * SLOTS
    now = pl.program_id(0)
    block = packs * keys

    def fetch(i):
        rows = pl.ds(pl.multiple_of((first + i) * block, block), block)
        return [
            pltpu.make_async_copy(sk_all.at[rows, :], sk_held.at[i], sem.at[0, i]),
            pltpu.make_async_copy(sv_all.at[rows, :], sv_held.at[i], sem.at[1, i]),
        ]

    @pl.when(now == 0)
    def _():
        for i in range(sk_held.shape[0]):
            for copy in fetch(i):
                copy.start()

    for copy in fetch(now):
        copy.wait()
    sk_ref, sv_ref = sk_held.at[now], sv_held.at[now]
    row = lax.broadcasted_iota(jnp.int32, (PACK, keys), 0)
    col = lax.broadcasted_iota(jnp.int32, (PACK, keys), 1)
    owner = (row >> 2) & 3
    same = owner == (col >> 6)
    slot = col & (SLOTS - 1)
    row_n = lax.broadcasted_iota(jnp.int32, (PACK, TOK), 0)
    col_n = lax.broadcasted_iota(jnp.int32, (PACK, TOK), 1)
    same_n = (((row_n >> 2) & 3) == (col_n >> 2)) & ((col_n & 3) <= (row_n & 3))

    def scores(g):
        block = q_ref[g * per : (g + 1) * per, :, :].astype(jnp.float32)
        block = block.reshape(TOK, GROUP * HD).astype(jnp.bfloat16)
        q = jnp.concatenate([block[:, h * HD : (h + 1) * HD] for h in range(GROUP)], axis=0)
        qp_ref[g * PACK : (g + 1) * PACK, :] = q
        return dot_t(q, sk_ref[g * keys : (g + 1) * keys, :]), dot_t(q, nk_ref[g * TOK : (g + 1) * TOK, :])

    ahead = scores(0)
    for g in range(packs):
        s, s_n = ahead
        if g + 1 < packs:
            ahead = scores(g + 1)
        rows = pl.ds(g * PACK, PACK)
        length = jnp.full((PACK, keys), len_ref[(base + g) * per], jnp.int32)
        for j in range(1, per):
            length = jnp.where(owner == j, len_ref[(base + g) * per + j], length)
        s = jnp.where(same & (slot < length), s * SCALE, LOW)
        s_n = jnp.where(same_n, s_n * SCALE, LOW)
        m = jnp.maximum(row_max(s), jnp.max(s_n, axis=1, keepdims=True))
        p = jnp.exp2(s - m).astype(jnp.bfloat16)
        p_n = jnp.exp2(s_n - m).astype(jnp.bfloat16)
        new_v = nv_ref[g * TOK : (g + 1) * TOK, :]
        m_ref[rows, :] = jnp.broadcast_to(m, (PACK, HD))
        acc_ref[rows, :] = dot(p, with_ones(sv_ref[g * keys : (g + 1) * keys, :])) + dot(p_n, with_ones(new_v))


def suffix(q, sk, sv, nk, nv, lengths, later, half, state=()):
    rows = q.shape[0] * STEPS * GROUP
    grid = 2
    first = half * grid
    part = lambda a: pl.BlockSpec((a.shape[0] // (2 * grid),) + a.shape[1:], lambda i: (first + i,) + (0,) * (len(a.shape) - 1))
    outs = [
        jax.ShapeDtypeStruct((rows, HD), jnp.bfloat16),
        jax.ShapeDtypeStruct((rows, HD), jnp.float32),
        jax.ShapeDtypeStruct((rows, 2 * HD), jnp.float32),
    ]
    return pl.pallas_call(
        lambda *refs: suffix_body(first, *refs),
        grid=(grid,),
        in_specs=[part(a) for a in (q, nk, nv)]
        + [pl.BlockSpec(memory_space=pltpu.HBM)] * 2
        + [pl.BlockSpec(memory_space=pltpu.SMEM)]
        + [pl.BlockSpec(memory_space=pl.ANY)] * (1 + len(state)),
        out_specs=[part(o) for o in outs],
        out_shape=outs,
        input_output_aliases={7 + i: i for i in range(len(state))},
        scratch_shapes=[pltpu.VMEM((grid, sk.shape[0] // (2 * grid), HD), jnp.bfloat16)] * 2 + [pltpu.SemaphoreType.DMA((2, grid))],
        cost_estimate=pl.CostEstimate(flops=2_000_000_000, bytes_accessed=3_000_000, transcendentals=300_000),
        compiler_params=pltpu.CompilerParams(vmem_limit_bytes=12 * MIB),
        name="suffix",
    )(q, nk, nv, sk, sv, lengths, later, *state)


def attend(q, m, acc, kvs, emit, tile=512):
    tiles = q.shape[0] // tile
    scores = lambda i: [dot_t(q[i * tile : (i + 1) * tile, :], kv[:, :HD]) for kv in kvs]
    ahead = scores(0)
    for i in range(tiles):
        parts = ahead
        if i + 1 < tiles:
            ahead = scores(i + 1)
        rows = slice(i * tile, (i + 1) * tile)
        top = row_max(parts[0])
        for s in parts[1:]:
            top = jnp.maximum(top, row_max(s))
        old = m[rows, :]
        new = jnp.maximum(old, top * SCALE)
        out = acc[rows, :] * wide(jnp.exp2(old - new), 2)
        for s, kv in zip(parts, kvs):
            p = jnp.exp2(s * SCALE - wide(new, s.shape[1] // HD)).astype(jnp.bfloat16)
            out = out + dot(p, with_ones(kv[:, HD:]))
        emit(i, rows, new, out)


def prefix_body(n, *refs):
    m_out, acc_out = refs[3 + n :]

    def emit(_, rows, new, out):
        m_out[rows, :] = new
        acc_out[rows, :] = out

    attend(refs[0], refs[1], refs[2], refs[3 : 3 + n], emit)


def prefix(q, m, acc, kvs, tile=1024):
    rows = q.shape[0]
    part = lambda a: pl.BlockSpec((tile, a.shape[1]), lambda i: (i, 0))
    whole = lambda a: pl.BlockSpec(a.shape, lambda i: (0, 0))
    keys = sum(kv.shape[0] for kv in kvs)
    return pl.pallas_call(
        lambda *refs: prefix_body(len(kvs), *refs),
        grid=(rows // tile,),
        in_specs=[part(q), part(m), part(acc)] + [whole(kv) for kv in kvs],
        out_specs=[part(m), part(acc)],
        out_shape=[jax.ShapeDtypeStruct(m.shape, m.dtype), jax.ShapeDtypeStruct(acc.shape, acc.dtype)],
        cost_estimate=pl.CostEstimate(flops=rows * keys * HD * 8, bytes_accessed=7_000_000, transcendentals=rows * keys),
        compiler_params=pltpu.CompilerParams(vmem_limit_bytes=24 * MIB),
        name="prefix",
    )(q, m, acc, *kvs)


def final_body(n, *refs):
    weight_ref, mine_ref, other_ref, heads_ref = refs[3 + n :]

    def emit(i, rows, _, out):
        heads = (out[:, :HD] / out[:, HD:]).astype(jnp.bfloat16)
        packs = heads.shape[0] // PACK
        for g in range(packs):
            for h in range(GROUP):
                first = g * PACK + h * TOK
                to = (i * packs + g) * TOK
                heads_ref[to : to + TOK, h * HD : (h + 1) * HD] = heads[first : first + TOK, :]

    attend(refs[0], refs[1], refs[2], refs[3 : 3 + n], emit)
    heads = heads_ref[...]
    requests, steps, half = mine_ref.shape
    core = lax.axis_index("core")
    width = 512
    for ref, side in ((other_ref, 1 - core), (mine_ref, core)):
        for j in range(0, half, width):
            columns = pl.ds(pl.multiple_of(side * half + j, width), width)
            terms = dot(heads, weight_ref[:, columns])
            ref[:, :, j : j + width] = terms.reshape(requests, steps, width).astype(ref.dtype)


def final(q, m, acc, kvs, weight, part, parts):
    rows = q.shape[0] // parts
    tokens, half = rows // GROUP, weight.shape[1] // 2
    keys = sum(kv.shape[0] for kv in kvs)
    whole = lambda a: pl.BlockSpec(a.shape, lambda i: (0,) * len(a.shape))
    shape = (tokens // STEPS, STEPS, half)
    outs = [jax.ShapeDtypeStruct(shape, jnp.float32), jax.ShapeDtypeStruct(shape, jnp.bfloat16)]
    return pl.pallas_call(
        lambda *refs: final_body(len(kvs), *refs),
        grid=(1,),
        in_specs=[pl.BlockSpec((rows, a.shape[1]), lambda i: (part, 0)) for a in (q, m, acc)]
        + [whole(kv) for kv in kvs]
        + [pl.BlockSpec(memory_space=pltpu.VMEM)],
        out_specs=[whole(o) for o in outs],
        out_shape=outs,
        scratch_shapes=[pltpu.VMEM((tokens, GROUP * HD), jnp.bfloat16)],
        cost_estimate=pl.CostEstimate(
            flops=rows * keys * HD * 8 + 8 * tokens * weight.size, bytes_accessed=12_000_000, transcendentals=rows * keys
        ),
        compiler_params=pltpu.CompilerParams(vmem_limit_bytes=24 * MIB),
        name="final",
    )(q, m, acc, *kvs, weight)


def place_body(n, lows, *refs):
    out_ref, sem = refs[-2:]
    half = refs[0].shape[2]
    core = lax.axis_index("core")
    copies = []
    for i in range(n):
        side = core if i % 2 == 0 else 1 - core
        rows = pl.ds(lows[i // 2], refs[i].shape[0])
        columns = pl.ds(pl.multiple_of(side * half, half), half)
        copies.append(pltpu.make_async_copy(refs[i], out_ref.at[rows, :, columns], sem.at[i]))
    for copy in copies:
        copy.start()
    for copy in copies:
        copy.wait()


def place(pieces, lows, shape):
    n = len(pieces)
    return pl.pallas_call(
        lambda *refs: place_body(n, lows, *refs),
        in_specs=[pl.BlockSpec(memory_space=pltpu.VMEM)] * n,
        out_specs=pl.BlockSpec(memory_space=pl.ANY),
        out_shape=jax.ShapeDtypeStruct(shape, pieces[0].dtype),
        scratch_shapes=[pltpu.SemaphoreType.DMA((n,))],
        compiler_params=pltpu.CompilerParams(vmem_limit_bytes=2 * MIB),
        name="place",
    )(*pieces)


def local(queries, prefix_keys, prefix_values, suffix_keys, suffix_values, new_keys, new_values, suffix_lengths, out_weight):
    requests = queries.shape[0]
    even = lambda a: lax.ppermute(a, "z", E_PAIRS)
    skip = lambda a: lax.ppermute(a, "z", SKIP_PAIRS)
    odd = lambda a: lax.ppermute(a, "z", O_PAIRS)
    x1 = lambda a: lax.ppermute(a, "x", [(i, i ^ 1) for i in range(4)])
    x3 = lambda a: lax.ppermute(a, "x", [(i, i ^ 3) for i in range(4)])
    y = lambda a: lax.ppermute(a, "ylo", [(0, 1), (1, 0)])
    swap_core = lambda a: lax.ppermute(a, "core", [(0, 1), (1, 0)])
    swap_y = lambda a: lax.ppermute(a, "yhi", [(0, 1), (1, 0)])

    flat = lambda a: a.reshape(-1, a.shape[-1])
    args = [queries] + [flat(a) for a in (suffix_keys, suffix_values, new_keys, new_values)]
    after = lambda a, b: lax.optimization_barrier((a, b))[0]

    own = glue(pack_body, prefix_keys.shape[0], 2_000_000_000, prefix_keys, prefix_values)
    pair = glue(join_body, 2 * own.shape[0], 10_000_000_000, own, even(prefix_keys), even(prefix_values))
    state = suffix(*args, suffix_lengths, pair, 0)
    r2 = after(odd(pair), state[1])
    q, m, acc = suffix(*args, suffix_lengths, r2, 1, state)
    r3, r4 = even(r2), after(skip(r2), m)
    line = jnp.concatenate([pair, r2, r3, r4], axis=0)
    b_x1, b_x3, b_y = x1(line), x3(line), y(line)
    m, acc = prefix(q, m, acc, [line])
    sent_y = after(b_y, m)
    b_yx1, b_yx3 = x1(sent_y), x3(sent_y)
    m, acc = prefix(q, m, acc, [b_y, b_x3])
    b_far, b_yfar = x1(after(b_x3, (b_yx1, m))), x3(after(b_yx1, m))
    m, acc = prefix(q, m, acc, [b_x1, b_yx1, b_yx3])

    shape = (requests, STEPS, out_weight.shape[1])
    last = [b_far, b_yfar]
    mine, other = final(q, m, acc, last, out_weight, 0, 2)
    mine_b, other_b = final(q, m, acc, last, out_weight, 1, 2)
    got = after(swap_core(other), mine_b)
    combine = lambda mine, got: (mine + got.astype(jnp.float32)).astype(jnp.bfloat16)
    cut = lambda a, sizes: [a[sum(sizes[:i]) : sum(sizes[: i + 1])] for i in range(len(sizes))]
    low = requests // 4
    pieces = [combine(mine[:low], got[:low])]
    pieces += [combine(mine[low:], after(got, pieces[0])[low:])]
    pieces += cut(combine(mine_b, swap_core(after(other_b, pieces[0]))), (24, 8))
    moved = [swap_y(piece) for piece in pieces]
    moved[:3] = lax.optimization_barrier(moved[:3])
    halves, lows = [], [0]
    for piece, got in zip(pieces, moved):
        total = piece + got
        halves += [total, swap_core(total)]
        lows.append(lows[-1] + piece.shape[0])
    return place(halves, lows[:-1], shape)


def solution(mesh):
    fine = Mesh(mesh.devices.reshape(2, 4, 8, 2, 2), ("ylo", "x", "z", "yhi", "core"))
    req, tp = ("ylo", "x", "z"), ("yhi", "core")
    in_specs = (
        P(req, None, tp),
        P(req, tp),
        P(req, tp),
        P(req, None, tp),
        P(req, None, tp),
        P(req, None, tp),
        P(req, None, tp),
        P(req),
        P(tp, None),
    )
    return jax.shard_map(local, mesh=fine, in_specs=in_specs, out_specs=P(req, None, None), check_vma=False)
```
